512 devices in a mesh: gx: 32 (over y, x), yz: 16 (over z, core).
Axes of the slice: x: 4, y: 8, z: 8, core: 2. Of those that a mesh axis runs over, the one named last changes fastest.
Arguments:
- thermal_state_initial: float32 [1024, 1024, 128], P('gx', 'yz'), may hold values from -5 to 5
- x_conductance_scaled: float32 [1024, 1024, 128], P('gx', 'yz'), may hold values from 30000 to 100000
- y_conductance_scaled: float32 [1024, 128], P('yz'), may hold values from 0.05 to 0.4
- z_conductance_scaled: float32 [1024, 128], P('yz'), may hold values from 0.05 to 0.4
Outputs:
- updated: float32 [1024, 1024, 128], P('gx', 'yz')
The draws below stay inside these ranges and needn't reach their ends.
All inputs are finite; a program needn't handle non-finite values.
Results may differ from the reference program's by a relative error of at most 0.00055.
Values sent between devices are 32-bit elements; how exact they have to be, the bound alone decides.
A program may use at most 64 MiB of HBM per device.

```python
import math
import jax
import jax.numpy as jnp
from jax import lax

NX = 1024
NY = 1024
NZ = 128


def draw_thermal_state_initial(key, part):
    key = jax.random.fold_in(key, 11)
    key_smooth, key_rough = jax.random.split(key)
    position = jnp.arange(NX, dtype=jnp.float32) / NX
    amplitude = jnp.clip(jax.random.normal(key_smooth, (NY, NZ), jnp.float32), -3.0, 3.0)
    profile = jnp.cos(1.5 * jnp.pi * position)
    rough = 0.3 * jnp.clip(jax.random.normal(key_rough, (NX, NY, NZ), jnp.float32), -3.0, 3.0)
    return profile[:, None, None] * amplitude[None] + rough


def level_of(own_key, extent, cuts, low, largest):
    def one(dim, shards_of):
        heights = jax.random.uniform(jax.random.fold_in(jax.random.fold_in(own_key, 6), dim), (shards_of,), jnp.float32, low / len(cuts), largest / len(cuts))
        return jnp.repeat(jnp.exp(heights), extent[dim] // shards_of).reshape((-1,) + (1,) * (len(extent) - dim - 1))

    gain = one(*cuts[0])
    for cut in cuts[1:]:
        gain = gain * one(*cut)
    return gain


def setup_inputs(seed: int = 0) -> dict:
    key_of = jax.random.split(jax.random.key(seed), 5)
    thermal_state_initial = draw_thermal_state_initial(jax.random.fold_in(key_of[4], 71), 0)
    x_conductance_scaled = jnp.clip(jnp.exp(math.log(100000.0) - 1.2039728 * jax.random.uniform(key_of[1], (NX, NY, NZ), jnp.float32) ** level_of(key_of[1], (NX, NY, NZ), ((0, 32), (1, 16)), -0.2, 0.2)), 30000.0, 100000.0)
    y_conductance_scaled = jnp.clip(jnp.exp(math.log(0.4) - 2.0794415 * jax.random.uniform(key_of[2], (NY, NZ), jnp.float32) ** level_of(key_of[2], (NY, NZ), ((0, 16),), -0.2, 0.2)), 0.05, 0.4)
    z_conductance_scaled = jnp.clip(jnp.exp(math.log(0.4) - 2.0794415 * jax.random.uniform(key_of[3], (NY, NZ), jnp.float32) ** level_of(key_of[3], (NY, NZ), ((0, 16),), -0.2, 0.2)), 0.05, 0.4)
    return dict(thermal_state_initial=thermal_state_initial, x_conductance_scaled=x_conductance_scaled, y_conductance_scaled=y_conductance_scaled, z_conductance_scaled=z_conductance_scaled)


def arriving_upward(values, dimension):
    border = jnp.zeros_like(lax.slice_in_dim(values, 0, 1, axis=dimension))
    inner = lax.slice_in_dim(values, 0, values.shape[dimension] - 1, axis=dimension)
    return jnp.concatenate([border, inner], dimension)


def arriving_downward(values, dimension):
    border = jnp.zeros_like(lax.slice_in_dim(values, 0, 1, axis=dimension))
    inner = lax.slice_in_dim(values, 1, values.shape[dimension], axis=dimension)
    return jnp.concatenate([inner, border], dimension)


def reference(thermal_state_initial, x_conductance_scaled, y_conductance_scaled, z_conductance_scaled):
    y_coupling_higher = arriving_downward(y_conductance_scaled, 0)
    z_coupling_higher = arriving_downward(z_conductance_scaled, 1)
    highest_position_id = NX - 1

    def row_terms(stripe_position_id):
        middle_field_values = lax.dynamic_index_in_dim(thermal_state_initial, stripe_position_id, 0, keepdims=False)
        previous_position_id = jnp.maximum(stripe_position_id - 1, 0).astype(jnp.int32)
        following_position_id = jnp.minimum(stripe_position_id + 1, highest_position_id).astype(jnp.int32)
        stripe_arriving_upward = jnp.where(stripe_position_id > 0, lax.dynamic_index_in_dim(thermal_state_initial, previous_position_id, 0, keepdims=False), 0.0)
        stripe_arriving_downward = jnp.where(stripe_position_id < highest_position_id, lax.dynamic_index_in_dim(thermal_state_initial, following_position_id, 0, keepdims=False), 0.0)
        coupling_smaller_side = lax.dynamic_index_in_dim(x_conductance_scaled, stripe_position_id, 0, keepdims=False)
        coupling_larger_side = jnp.where(stripe_position_id < highest_position_id, lax.dynamic_index_in_dim(x_conductance_scaled, following_position_id, 0, keepdims=False), 0.0)
        thermal_current_x = coupling_smaller_side * (middle_field_values - stripe_arriving_upward) + coupling_larger_side * (middle_field_values - stripe_arriving_downward)
        thermal_current_y = y_conductance_scaled * (middle_field_values - arriving_upward(middle_field_values, 0)) + y_coupling_higher * (middle_field_values - arriving_downward(middle_field_values, 0))
        thermal_current_z = z_conductance_scaled * (middle_field_values - arriving_upward(middle_field_values, 1)) + z_coupling_higher * (middle_field_values - arriving_downward(middle_field_values, 1))
        forcing_contribution = middle_field_values - 0.5 * thermal_current_x - thermal_current_y - thermal_current_z
        lower_coef = 0.5 * coupling_smaller_side
        upper_coef = 0.5 * coupling_larger_side
        return lower_coef, 1.0 + lower_coef + upper_coef, upper_coef, forcing_contribution

    def forward(state_pair, stripe_position_id):
        factor_prev, partial_prev = state_pair
        lower_coef, diagonal, upper_coef, forcing_contribution = row_terms(stripe_position_id)
        divisor = diagonal - lower_coef * factor_prev
        factor = upper_coef / divisor
        partial_value = (forcing_contribution + lower_coef * partial_prev) / divisor
        return (factor, partial_value), (factor, partial_value)

    blank_plane = jnp.zeros((NY, NZ), jnp.float32)
    _, (factors, partials) = lax.scan(forward, (blank_plane, blank_plane), jnp.arange(NX, dtype=jnp.int32))

    def backward(following, row_pair):
        factor, partial_value = row_pair
        solution_row = partial_value + factor * following
        return solution_row, solution_row

    _, solved = lax.scan(backward, blank_plane, (factors, partials), reverse=True)
    return solved
```

```python
import functools

import jax
import jax.numpy as jnp
from jax import lax
from jax.experimental import pallas as pl
from jax.experimental.pallas import tpu as pltpu
from jax.sharding import PartitionSpec as P

MESH = pl.DeviceIdType.MESH
F32 = jnp.float32

NG = 32
NYZ = 16
GY, GX = 8, 4
L = 32
ROWS = 64
TILES = ROWS // 8
SOLVERS = (4, 1, 3, 5, 7, 29, 31, 28)


def ring_distance(a, n):
    return min(a, n - a)


OFFSETS = sorted(
    [(dy, dx) for dy in range(GY) for dx in range(GX) if (dy, dx) != (0, 0)],
    key=lambda o: -(ring_distance(o[0], GY) + ring_distance(o[1], GX)),
)


def reciprocal(x):
    g = pl.reciprocal(x, approx=True)
    return g * (2.0 - x * g)


def sweep_kernel(
    u_hbm, k_hbm, ky_hbm, kz_hbm, out_hbm,
    u, k, ky, kz, fl, fr, g, rg, edge, coef,
    send_up, send_down, from_below, from_above,
    a_send, a_recv, w_send, w_recv, out,
    load_sem, halo_send_sem, halo_recv_sem,
    a_send_sem, a_recv_sem, w_send_sem, w_recv_sem, store_sem,
):
    me = lax.axis_index("gx")
    z = lax.axis_index("yz")
    is_solver = functools.reduce(jnp.logical_or, [me == s for s in SOLVERS])
    tile = sum(jnp.where(me == s, t, 0) for t, s in enumerate(SOLVERS))
    row0 = pl.multiple_of(tile * 8, 8)
    barrier = pltpu.get_barrier_semaphore()

    pieces = [
        (u_hbm.at[:, pl.ds(0, 8)], u.at[:, pl.ds(0, 8)]),
        (u_hbm.at[:, pl.ds(56, 8)], u.at[:, pl.ds(56, 8)]),
        (ky_hbm, ky),
        (k_hbm, k),
        (u_hbm.at[:, pl.ds(8, 48)], u.at[:, pl.ds(8, 48)]),
        (kz_hbm, kz),
    ]
    loads = [pltpu.make_async_copy(s, d, load_sem.at[i]) for i, (s, d) in enumerate(pieces)]
    for c in loads:
        c.start()

    @pl.when(z > 0)
    def _():
        pl.semaphore_signal(barrier, inc=1, device_id=(me, z - 1), device_id_type=MESH)

    @pl.when(z < NYZ - 1)
    def _():
        pl.semaphore_signal(barrier, inc=1, device_id=(me, z + 1), device_id_type=MESH)

    my, mx = me // GX, me % GX

    def other(o):
        return lax.rem(my + o[0], GY) * GX + lax.rem(mx + o[1], GX)

    @pl.when(is_solver)
    def _():
        for o in OFFSETS:
            pl.semaphore_signal(barrier, inc=1, device_id=(other(o), z), device_id_type=MESH)

    loads[0].wait()
    loads[1].wait()
    loads[2].wait()
    for i in range(L):
        send_up[pl.ds(i, 1), :] = u[i, pl.ds(63, 1), :]
        send_down[pl.ds(i, 1), :] = u[i, pl.ds(0, 1), :]
    send_down[pl.ds(32, 8), :] = jnp.broadcast_to(ky[pl.ds(0, 1), :], (8, 128))
    greeted = jnp.where(z > 0, 1, 0) + jnp.where(z < NYZ - 1, 1, 0)
    greeted = greeted + jnp.where(is_solver, len(SOLVERS) - 1, len(SOLVERS))
    pl.semaphore_wait(barrier, greeted)

    up = pltpu.make_async_remote_copy(
        src_ref=send_up, dst_ref=from_below, send_sem=halo_send_sem.at[0],
        recv_sem=halo_recv_sem.at[0], device_id=(me, z + 1), device_id_type=MESH,
    )
    down = pltpu.make_async_remote_copy(
        src_ref=send_down, dst_ref=from_above, send_sem=halo_send_sem.at[1],
        recv_sem=halo_recv_sem.at[1], device_id=(me, z - 1), device_id_type=MESH,
    )

    @pl.when(z < NYZ - 1)
    def _():
        up.start()

    @pl.when(z > 0)
    def _():
        down.start()

    @pl.when(z == 0)
    def _():
        from_below[...] = jnp.zeros((L, 128), F32)

    @pl.when(z == NYZ - 1)
    def _():
        from_above[...] = jnp.zeros((L + 8, 128), F32)

    loads[3].wait()
    zero = jnp.zeros((ROWS, 128), F32)

    def eliminate(i, state):
        link, mass, mass_p = state
        k_next = 0.5 * k[i]
        gi = reciprocal((k_next + mass) + link)
        left = link * gi
        right = k_next * gi
        fl[i - 1] = left
        fr[i - 1] = right
        g[i - 1] = gi
        return link * right, 1.0 + right * mass, mass_p + left * mass

    link, mass, mass_p = lax.fori_loop(1, L, eliminate, (0.5 * k[0], zero + 1.0, zero))
    for t in range(TILES):
        rows = slice(8 * t, 8 * t + 8)
        a_send[t, 0] = mass_p[rows]
        a_send[t, 1] = mass[rows]
        a_send[t, 2] = link[rows]

    loads[4].wait()
    loads[5].wait()
    row = lax.broadcasted_iota(jnp.int32, (ROWS, 128), 0)
    lane = lax.broadcasted_iota(jnp.int32, (ROWS, 128), 1)
    kya = jnp.where(row == ROWS - 1, 0.0, pltpu.roll(ky[...], ROWS - 1, 0))
    kza = jnp.where(lane == 127, 0.0, pltpu.roll(kz[...], 127, 1))
    coef[0] = 2.0 - ky[...] - kya - kz[...] - kza
    coef[1] = jnp.where(row == 0, 0.0, ky[...])
    coef[2] = kya
    coef[3] = jnp.where(lane == 0, 0.0, kz[...])
    coef[4] = kza

    def rhs(i):
        v = u[i]
        b = coef[0] * v
        b = b + coef[1] * pltpu.roll(v, 1, 0) + coef[2] * pltpu.roll(v, ROWS - 1, 0)
        b = b + coef[3] * pltpu.roll(v, 1, 1) + coef[4] * pltpu.roll(v, 127, 1)
        edge[i, pl.ds(0, 8)] = b[0:8]
        edge[i, pl.ds(8, 8)] = b[56:64]
        return b

    mid = pl.ds(8, 48)

    def source(i, state):
        r, r_p = state
        r = rhs(i)[8:56] + fr[i - 1, mid] * r
        rg[i, mid] = r * g[i, mid]
        return r, r_p + fl[i, mid] * r

    r = rhs(0)[8:56]
    rg[0, mid] = r * g[0, mid]
    r, r_p = lax.fori_loop(1, L - 1, source, (r, fl[0, mid] * r))
    r = rhs(L - 1)[8:56] + fr[L - 2, mid] * r
    for t in range(1, TILES - 1):
        rows = slice(8 * t - 8, 8 * t)
        a_send[t, 3] = r_p[rows]
        a_send[t, 4] = r[rows]

    def send_tile(t):
        @pl.when(me != SOLVERS[t])
        def _():
            pltpu.make_async_remote_copy(
                src_ref=a_send.at[t], dst_ref=a_recv.at[me], send_sem=a_send_sem,
                recv_sem=a_recv_sem, device_id=(SOLVERS[t], z), device_id_type=MESH,
            ).start()

        @pl.when(me == SOLVERS[t])
        def _():
            a_recv[me] = a_send[t]

    for t in range(TILES - 2, 0, -1):
        send_tile(t)

    @pl.when(z > 0)
    def _():
        up.wait_recv()

    @pl.when(z < NYZ - 1)
    def _():
        down.wait_recv()

    row8 = lax.broadcasted_iota(jnp.int32, (8, 128), 0)
    c_first = jnp.where(row8 == 0, jnp.broadcast_to(ky[pl.ds(0, 1), :], (8, 128)), 0.0)
    c_last = jnp.where(row8 == 7, from_above[pl.ds(32, 8), :], 0.0)
    first, last = pl.ds(0, 8), pl.ds(56, 8)

    def edge_rhs(i):
        b_first = edge[i, pl.ds(0, 8)] + c_first * from_below[pl.ds(i, 1), :]
        b_last = edge[i, pl.ds(8, 8)] + c_last * (from_above[pl.ds(i, 1), :] - u[i, last])
        return b_first, b_last

    def edge_source(i, state):
        r0, r7, p0, p7 = state
        b0, b7 = edge_rhs(i)
        r0 = b0 + fr[i - 1, first] * r0
        r7 = b7 + fr[i - 1, last] * r7
        rg[i, first] = r0 * g[i, first]
        rg[i, last] = r7 * g[i, last]
        return r0, r7, p0 + fl[i, first] * r0, p7 + fl[i, last] * r7

    r0, r7 = edge_rhs(0)
    rg[0, first] = r0 * g[0, first]
    rg[0, last] = r7 * g[0, last]
    r0, r7, p0, p7 = lax.fori_loop(
        1, L - 1, edge_source, (r0, r7, fl[0, first] * r0, fl[0, last] * r7)
    )
    b0, b7 = edge_rhs(L - 1)
    a_send[0, 3] = p0
    a_send[0, 4] = b0 + fr[L - 2, first] * r0
    a_send[TILES - 1, 3] = p7
    a_send[TILES - 1, 4] = b7 + fr[L - 2, last] * r7
    send_tile(0)
    send_tile(TILES - 1)

    @pl.when(is_solver)
    def _():
        landed = a_recv.at[pl.ds(0, NG - 1)]
        pltpu.make_async_copy(landed, landed, a_recv_sem).wait()
        masses = [a_recv[d, 1] + (a_recv[d + 1, 0] if d < NG - 1 else 0.0) for d in range(NG)]
        sources = [a_recv[d, 4] + (a_recv[d + 1, 3] if d < NG - 1 else 0.0) for d in range(NG)]
        links = [a_recv[d, 2] for d in range(NG)]
        ids = list(range(NG))
        levels = []
        while len(ids) > 1:
            gone = []
            new_links = []
            for j in range(0, len(ids), 2):
                gi = reciprocal((links[j] + links[j + 1]) + masses[j])
                left, right = links[j] * gi, links[j + 1] * gi
                gone.append((ids[j], left, right, sources[j] * gi))
                if j > 0:
                    masses[j - 1] = masses[j - 1] + left * masses[j]
                    sources[j - 1] = sources[j - 1] + left * sources[j]
                masses[j + 1] = masses[j + 1] + right * masses[j]
                sources[j + 1] = sources[j + 1] + right * sources[j]
                new_links.append(links[j] * right)
            levels.append((gone, ids[1::2]))
            ids, masses, sources, links = ids[1::2], masses[1::2], sources[1::2], new_links
        w = {-1: jnp.zeros((8, 128), F32), ids[0]: sources[0] * reciprocal(masses[0] + links[0])}
        for gone, kept in reversed(levels):
            for j, (d, left, right, part) in enumerate(gone):
                below = kept[j - 1] if j > 0 else -1
                w[d] = left * w[below] + right * w[kept[j]] + part
        for d in range(-1, NG):
            w_send[d + 1] = w[d]
        for o in OFFSETS:
            d = other(o)
            pltpu.make_async_remote_copy(
                src_ref=w_send.at[pl.ds(d, 2)], dst_ref=w_recv.at[:, pl.ds(row0, 8)],
                send_sem=w_send_sem, recv_sem=w_recv_sem, device_id=(d, z), device_id_type=MESH,
            ).start()
        w_recv[:, pl.ds(row0, 8), :] = w_send[pl.ds(me, 2)]
        landed = w_recv.at[:, pl.ds(0, ROWS - 8)]
        pltpu.make_async_copy(landed, landed, w_recv_sem).wait()

    @pl.when(jnp.logical_not(is_solver))
    def _():
        pltpu.make_async_copy(w_recv, w_recv, w_recv_sem).wait()

    w_p = w_recv[0]
    w_last = w_recv[1]
    out[L - 1] = w_last - u[L - 1]
    chunk = 8

    def back(j, w):
        i = L - 2 - j
        w = (fl[i] * w_p + rg[i]) + fr[i] * w
        out[i] = w - u[i]
        return w

    w = w_last
    stores = []
    for c in range(L // chunk):
        low = c * chunk - (1 if c > 0 else 0)
        w = lax.fori_loop(low, (c + 1) * chunk - 1, back, w)
        part = pl.ds(L - chunk * (c + 1), chunk)
        stores.append(pltpu.make_async_copy(out.at[part], out_hbm.at[part], store_sem.at[c]))
        stores[-1].start()

    @pl.when(z < NYZ - 1)
    def _():
        up.wait_send()

    @pl.when(z > 0)
    def _():
        down.wait_send()

    @pl.when(is_solver)
    def _():
        sent = a_send.at[pl.ds(0, TILES - 1)]
        pltpu.make_async_copy(sent, sent, a_send_sem).wait()
        sent = a_recv.at[pl.ds(0, NG - 1), pl.ds(0, 2)]
        pltpu.make_async_copy(sent, sent, w_send_sem).wait()

    @pl.when(jnp.logical_not(is_solver))
    def _():
        pltpu.make_async_copy(a_send, a_send, a_send_sem).wait()

    for c in stores:
        c.wait()


def shards(u, kx, ky, kz):
    field = pltpu.VMEM((L, ROWS, 128), F32)
    any_space = pl.BlockSpec(memory_space=pl.ANY)
    return pl.pallas_call(
        sweep_kernel,
        out_shape=jax.ShapeDtypeStruct((L, ROWS, 128), F32),
        in_specs=[any_space] * 4,
        out_specs=any_space,
        scratch_shapes=[
            field, field, pltpu.VMEM((ROWS, 128), F32), pltpu.VMEM((ROWS, 128), F32),
            field, field, field, field,
            pltpu.VMEM((L, 16, 128), F32), pltpu.VMEM((5, ROWS, 128), F32),
            pltpu.VMEM((L, 128), F32), pltpu.VMEM((L + 8, 128), F32),
            pltpu.VMEM((L, 128), F32), pltpu.VMEM((L + 8, 128), F32),
            pltpu.VMEM((TILES, 5, 8, 128), F32), pltpu.VMEM((NG, 5, 8, 128), F32),
            pltpu.VMEM((NG + 1, 8, 128), F32), pltpu.VMEM((2, ROWS, 128), F32),
            field,
            pltpu.SemaphoreType.DMA((6,)), pltpu.SemaphoreType.DMA((2,)),
            pltpu.SemaphoreType.DMA((2,)),
            pltpu.SemaphoreType.DMA, pltpu.SemaphoreType.DMA,
            pltpu.SemaphoreType.DMA, pltpu.SemaphoreType.DMA,
            pltpu.SemaphoreType.DMA((L // 8,)),
        ],
        compiler_params=pltpu.CompilerParams(
            collective_id=0, has_side_effects=True, vmem_limit_bytes=32 * 1024 * 1024
        ),
        name="implicit_sweep",
    )(u, kx, ky, kz)


def solution(mesh):
    return jax.shard_map(
        shards,
        mesh=mesh,
        in_specs=(P("gx", "yz", None), P("gx", "yz", None), P("yz", None), P("yz", None)),
        out_specs=P("gx", "yz", None),
        check_vma=False,
    )
```

```python
import functools

import jax
import jax.numpy as jnp
from jax import lax
from jax.experimental import pallas as pl
from jax.experimental.pallas import tpu as pltpu
from jax.sharding import PartitionSpec as P

MESH = pl.DeviceIdType.MESH
F32 = jnp.float32

NG = 32
NYZ = 16
GY, GX = 8, 4
L = 32
ROWS = 64
SLOTS = 16
WIDE = ROWS // SLOTS


def ring_distance(a, n):
    return min(a, n - a)


def distance_to_first(d):
    return ring_distance(d // GX, GY) + ring_distance(d % GX, GX)


SOLVERS = (4, 1, 3) + (2, 8, 24, 29) + tuple(d for d in range(NG) if distance_to_first(d) == 3) + (28,)


OFFSETS = sorted(
    [(dy, dx) for dy in range(GY) for dx in range(GX) if (dy, dx) != (0, 0)],
    key=lambda o: -(ring_distance(o[0], GY) + ring_distance(o[1], GX)),
)


def reciprocal(x):
    g = pl.reciprocal(x, approx=True)
    return g * (2.0 - x * g)


def sweep_kernel(
    u_hbm, k_hbm, ky_hbm, kz_hbm, out,
    u, k, ky, kz, fl, fr, g, rg, planes,
    send_up, send_down, from_below, from_above,
    a_send, a_recv, w_send, w_recv,
    load_sem, halo_send_sem, halo_recv_sem,
    a_send_sem, a_recv_sem, w_send_sem, w_recv_sem,
):
    me = lax.axis_index("gx")
    z = lax.axis_index("yz")
    is_solver = functools.reduce(jnp.logical_or, [me == s for s in SOLVERS])
    slot = sum(jnp.where(me == d, s, 0) for s, d in enumerate(SOLVERS))
    barrier = pltpu.get_barrier_semaphore()

    pieces = [
        (u_hbm.at[:, pl.ds(0, 8)], u.at[:, pl.ds(0, 8)]),
        (u_hbm.at[:, pl.ds(56, 8)], u.at[:, pl.ds(56, 8)]),
        (ky_hbm, ky),
        (k_hbm, k),
        (u_hbm.at[:, pl.ds(8, 48)], u.at[:, pl.ds(8, 48)]),
        (kz_hbm, kz),
    ]
    loads = [pltpu.make_async_copy(s, d, load_sem.at[i]) for i, (s, d) in enumerate(pieces)]
    for c in loads:
        c.start()

    @pl.when(z > 0)
    def _():
        pl.semaphore_signal(barrier, inc=1, device_id=(me, z - 1), device_id_type=MESH)

    @pl.when(z < NYZ - 1)
    def _():
        pl.semaphore_signal(barrier, inc=1, device_id=(me, z + 1), device_id_type=MESH)

    my, mx = me // GX, me % GX

    def other(o):
        return lax.rem(my + o[0], GY) * GX + lax.rem(mx + o[1], GX)

    @pl.when(is_solver)
    def _():
        for o in OFFSETS:
            pl.semaphore_signal(barrier, inc=1, device_id=(other(o), z), device_id_type=MESH)

    loads[0].wait()
    loads[1].wait()
    loads[2].wait()
    for i in range(L):
        send_up[pl.ds(i, 1), :] = u[i, pl.ds(63, 1), :]
        send_down[pl.ds(i, 1), :] = u[i, pl.ds(0, 1), :]
    send_down[pl.ds(32, 8), :] = jnp.broadcast_to(ky[pl.ds(0, 1), :], (8, 128))
    greeted = jnp.where(z > 0, 1, 0) + jnp.where(z < NYZ - 1, 1, 0)
    greeted = greeted + jnp.where(is_solver, len(SOLVERS) - 1, len(SOLVERS))
    pl.semaphore_wait(barrier, greeted)

    up = pltpu.make_async_remote_copy(
        src_ref=send_up, dst_ref=from_below, send_sem=halo_send_sem.at[0],
        recv_sem=halo_recv_sem.at[0], device_id=(me, z + 1), device_id_type=MESH,
    )
    down = pltpu.make_async_remote_copy(
        src_ref=send_down, dst_ref=from_above, send_sem=halo_send_sem.at[1],
        recv_sem=halo_recv_sem.at[1], device_id=(me, z - 1), device_id_type=MESH,
    )

    @pl.when(z < NYZ - 1)
    def _():
        up.start()

    @pl.when(z > 0)
    def _():
        down.start()

    @pl.when(z == 0)
    def _():
        from_below[...] = jnp.zeros((L, 128), F32)

    @pl.when(z == NYZ - 1)
    def _():
        from_above[...] = jnp.zeros((L + 8, 128), F32)

    def put(part, plane):
        for s in range(SLOTS):
            a_send[s, part] = plane[WIDE * s : WIDE * (s + 1)]

    loads[3].wait()
    zero = jnp.zeros((ROWS, 128), F32)

    def eliminate(i, state):
        link, mass, mass_p = state
        k_next = 0.5 * k[i]
        gi = reciprocal((k_next + mass) + link)
        left = link * gi
        right = k_next * gi
        fl[i - 1] = left
        fr[i - 1] = right
        g[i - 1] = gi
        return link * right, 1.0 + right * mass, mass_p + left * mass

    link, mass, mass_p = lax.fori_loop(1, L, eliminate, (0.5 * k[0], zero + 1.0, zero))
    put(0, mass_p)
    put(1, mass)
    put(2, link)

    loads[4].wait()
    loads[5].wait()
    row = lax.broadcasted_iota(jnp.int32, (ROWS, 128), 0)
    lane = lax.broadcasted_iota(jnp.int32, (ROWS, 128), 1)
    kya = jnp.where(row == ROWS - 1, 0.0, pltpu.roll(ky[...], ROWS - 1, 0))
    kza = jnp.where(lane == 127, 0.0, pltpu.roll(kz[...], 127, 1))
    planes[0] = 2.0 - ky[...] - kya - kz[...] - kza
    planes[1] = jnp.where(row == 0, 0.0, ky[...])
    planes[2] = kya
    planes[3] = jnp.where(lane == 0, 0.0, kz[...])
    planes[4] = kza

    def rhs(j, _):
        for i in range(4):
            i = 4 * j + i
            v = u[i]
            b = planes[0] * v
            b = b + planes[1] * pltpu.roll(v, 1, 0) + planes[2] * pltpu.roll(v, ROWS - 1, 0)
            rg[i] = b + planes[3] * pltpu.roll(v, 1, 1) + planes[4] * pltpu.roll(v, 127, 1)
        return 0

    lax.fori_loop(0, L // 4, rhs, 0)

    def source(i, state):
        r, r_p = state
        r = rg[i] + fr[i - 1] * r
        rg[i] = r * g[i]
        return r, r_p + fl[i] * r

    r = rg[0]
    rg[0] = r * g[0]
    r, r_p = lax.fori_loop(1, L - 1, source, (r, fl[0] * r))
    r = rg[L - 1] + fr[L - 2] * r
    put(3, r_p)
    put(4, r)

    def send_slot(s):
        @pl.when(me != SOLVERS[s])
        def _():
            pltpu.make_async_remote_copy(
                src_ref=a_send.at[s], dst_ref=a_recv.at[me], send_sem=a_send_sem,
                recv_sem=a_recv_sem, device_id=(SOLVERS[s], z), device_id_type=MESH,
            ).start()

        @pl.when(me == SOLVERS[s])
        def _():
            a_recv[me] = a_send[s]

    for s in range(SLOTS - 2, 0, -1):
        send_slot(s)

    @pl.when(z > 0)
    def _():
        up.wait_recv()

    @pl.when(z < NYZ - 1)
    def _():
        down.wait_recv()

    row8 = lax.broadcasted_iota(jnp.int32, (8, 128), 0)
    c_first = jnp.where(row8 == 0, jnp.broadcast_to(ky[pl.ds(0, 1), :], (8, 128)), 0.0)
    c_last = jnp.where(row8 == 7, from_above[pl.ds(32, 8), :], 0.0)
    first, last = pl.ds(0, 8), pl.ds(ROWS - 8, 8)

    def edge_rhs(i):
        b0 = c_first * from_below[pl.ds(i, 1), :]
        b7 = c_last * (from_above[pl.ds(i, 1), :] - u[i, last])
        return b0, b7

    def edge_source(i, state):
        r0, r7, p0, p7 = state
        b0, b7 = edge_rhs(i)
        r0 = b0 + fr[i - 1, first] * r0
        r7 = b7 + fr[i - 1, last] * r7
        rg[i, first] += r0 * g[i, first]
        rg[i, last] += r7 * g[i, last]
        return r0, r7, p0 + fl[i, first] * r0, p7 + fl[i, last] * r7

    r0, r7 = edge_rhs(0)
    rg[0, first] += r0 * g[0, first]
    rg[0, last] += r7 * g[0, last]
    r0, r7, p0, p7 = lax.fori_loop(
        1, L - 1, edge_source, (r0, r7, fl[0, first] * r0, fl[0, last] * r7)
    )
    b0, b7 = edge_rhs(L - 1)
    r0 = b0 + fr[L - 2, first] * r0
    r7 = b7 + fr[L - 2, last] * r7
    a_send[0, 3] += p0[:WIDE]
    a_send[0, 4] += r0[:WIDE]
    a_send[SLOTS - 1, 3] += p7[8 - WIDE :]
    a_send[SLOTS - 1, 4] += r7[8 - WIDE :]
    send_slot(0)
    send_slot(SLOTS - 1)

    @pl.when(is_solver)
    def _():
        landed = a_recv.at[pl.ds(0, NG - 1)]
        pltpu.make_async_copy(landed, landed, a_recv_sem).wait()
        masses = [a_recv[d, 1] + (a_recv[d + 1, 0] if d < NG - 1 else 0.0) for d in range(NG)]
        sources = [a_recv[d, 4] + (a_recv[d + 1, 3] if d < NG - 1 else 0.0) for d in range(NG)]
        links = [a_recv[d, 2] for d in range(NG)]
        ids = list(range(NG))
        levels = []
        while len(ids) > 1:
            gone = []
            new_links = []
            for j in range(0, len(ids), 2):
                gi = reciprocal((links[j] + links[j + 1]) + masses[j])
                left, right = links[j] * gi, links[j + 1] * gi
                gone.append((ids[j], left, right, sources[j] * gi))
                if j > 0:
                    masses[j - 1] = masses[j - 1] + left * masses[j]
                    sources[j - 1] = sources[j - 1] + left * sources[j]
                masses[j + 1] = masses[j + 1] + right * masses[j]
                sources[j + 1] = sources[j + 1] + right * sources[j]
                new_links.append(links[j] * right)
            levels.append((gone, ids[1::2]))
            ids, masses, sources, links = ids[1::2], masses[1::2], sources[1::2], new_links
        w = {-1: jnp.zeros((WIDE, 128), F32), ids[0]: sources[0] * reciprocal(masses[0] + links[0])}
        for gone, kept in reversed(levels):
            for j, (d, left, right, part) in enumerate(gone):
                below = kept[j - 1] if j > 0 else -1
                w[d] = left * w[below] + right * w[kept[j]] + part
        for d in range(-1, NG):
            w_send[d + 1] = w[d]
        for o in OFFSETS:
            d = other(o)
            pltpu.make_async_remote_copy(
                src_ref=w_send.at[pl.ds(d, 2)], dst_ref=w_recv.at[slot],
                send_sem=w_send_sem, recv_sem=w_recv_sem, device_id=(d, z), device_id_type=MESH,
            ).start()
        w_recv[slot] = w_send[pl.ds(me, 2)]
        landed = w_recv.at[pl.ds(0, SLOTS - 1)]
        pltpu.make_async_copy(landed, landed, w_recv_sem).wait()

    @pl.when(jnp.logical_not(is_solver))
    def _():
        pltpu.make_async_copy(w_recv, w_recv, w_recv_sem).wait()

    for s in range(SLOTS):
        planes[0, pl.ds(WIDE * s, WIDE)] = w_recv[s, 0]
        planes[1, pl.ds(WIDE * s, WIDE)] = w_recv[s, 1]
    w_p = planes[0]
    w_last = planes[1]
    out[L - 1] = w_last - u[L - 1]

    def back(j, w):
        i = L - 2 - j
        w = (fl[i] * w_p + rg[i]) + fr[i] * w
        out[i] = w - u[i]
        return w

    lax.fori_loop(0, L - 1, back, w_last)

    @pl.when(z < NYZ - 1)
    def _():
        up.wait_send()

    @pl.when(z > 0)
    def _():
        down.wait_send()

    @pl.when(is_solver)
    def _():
        sent = a_send.at[pl.ds(0, SLOTS - 1)]
        pltpu.make_async_copy(sent, sent, a_send_sem).wait()
        sent = a_recv.at[pl.ds(0, NG - 1), pl.ds(0, 2)]
        pltpu.make_async_copy(sent, sent, w_send_sem).wait()

    @pl.when(jnp.logical_not(is_solver))
    def _():
        pltpu.make_async_copy(a_send, a_send, a_send_sem).wait()


def shards(u, kx, ky, kz):
    field = pltpu.VMEM((L, ROWS, 128), F32)
    any_space = pl.BlockSpec(memory_space=pl.ANY)
    return pl.pallas_call(
        sweep_kernel,
        out_shape=pltpu.VMEM((L, ROWS, 128), F32),
        in_specs=[any_space] * 4,
        out_specs=pl.BlockSpec(memory_space=pltpu.VMEM),
        scratch_shapes=[
            field, field, pltpu.VMEM((ROWS, 128), F32), pltpu.VMEM((ROWS, 128), F32),
            field, field, field, field,
            pltpu.VMEM((5, ROWS, 128), F32),
            pltpu.VMEM((L, 128), F32), pltpu.VMEM((L + 8, 128), F32),
            pltpu.VMEM((L, 128), F32), pltpu.VMEM((L + 8, 128), F32),
            pltpu.VMEM((SLOTS, 5, WIDE, 128), F32), pltpu.VMEM((NG, 5, WIDE, 128), F32),
            pltpu.VMEM((NG + 1, WIDE, 128), F32), pltpu.VMEM((SLOTS, 2, WIDE, 128), F32),
            pltpu.SemaphoreType.DMA((6,)), pltpu.SemaphoreType.DMA((2,)),
            pltpu.SemaphoreType.DMA((2,)),
            pltpu.SemaphoreType.DMA, pltpu.SemaphoreType.DMA,
            pltpu.SemaphoreType.DMA, pltpu.SemaphoreType.DMA,
        ],
        compiler_params=pltpu.CompilerParams(
            collective_id=0, has_side_effects=True, vmem_limit_bytes=32 * 1024 * 1024
        ),
        name="implicit_sweep",
    )(*(pltpu.with_memory_space_constraint(a, pltpu.HBM) for a in (u, kx, ky, kz)))


def solution(mesh):
    return jax.shard_map(
        shards,
        mesh=mesh,
        in_specs=(P("gx", "yz", None), P("gx", "yz", None), P("yz", None), P("yz", None)),
        out_specs=P("gx", "yz", None),
        check_vma=False,
    )
```

```python
import functools

import jax
import jax.numpy as jnp
from jax import lax
from jax.experimental import pallas as pl
from jax.experimental.pallas import tpu as pltpu
from jax.sharding import PartitionSpec as P

MESH = pl.DeviceIdType.MESH
F32 = jnp.float32

NG = 32
NYZ = 16
GY, GX = 8, 4
L = 32
ROWS = 64
SLOTS = 16
WIDE = ROWS // SLOTS
PART = 8
STEP = 4


def ring_distance(a, n):
    return min(a, n - a)


SOLVERS = (4, 1, 3, 8, 24, 29, 6, 9, 11, 12, 20, 25, 27, 30, 5, 28)


OFFSETS = sorted(
    [(dy, dx) for dy in range(GY) for dx in range(GX) if (dy, dx) != (0, 0)],
    key=lambda o: -(ring_distance(o[0], GY) + ring_distance(o[1], GX)),
)


def reciprocal(x):
    g = pl.reciprocal(x, approx=True)
    return g * (2.0 - x * g)


def planes_loop(low, high, body, state):
    def step(j, state):
        for i in range(STEP):
            state = body(low + STEP * j + i, state)
        return state

    return lax.fori_loop(0, (high - low) // STEP, step, state)


def sweep_kernel(
    u_hbm, k_hbm, ky_hbm, kz_hbm, out,
    u, k, ky, kz, fl, fr, g, rg, planes,
    send_up, send_down, from_below, from_above,
    a_send, a_recv, w_send, w_recv,
    load_sem, halo_send_sem, halo_recv_sem,
    a_send_sem, a_recv_sem, w_send_sem, w_recv_sem,
):
    me = lax.axis_index("gx")
    z = lax.axis_index("yz")
    my, mx = me // GX, me % GX
    is_solver = functools.reduce(jnp.logical_or, [me == s for s in SOLVERS])
    slot = sum(jnp.where(me == d, s, 0) for s, d in enumerate(SOLVERS))
    barrier = pltpu.get_barrier_semaphore()

    parts = [pl.ds(c, PART) for c in range(0, L, PART)]
    pieces = [(k_hbm.at[c], k.at[c]) for c in parts] + [(ky_hbm, ky), (kz_hbm, kz)]
    pieces += [(u_hbm.at[c], u.at[c]) for c in parts]
    loads = [pltpu.make_async_copy(s, d, load_sem.at[i]) for i, (s, d) in enumerate(pieces)]
    for c in loads:
        c.start()
    first_y, first_u = len(parts), len(parts) + 2

    @pl.when(z > 0)
    def _():
        pl.semaphore_signal(barrier, inc=1, device_id=(me, z - 1), device_id_type=MESH)

    @pl.when(z < NYZ - 1)
    def _():
        pl.semaphore_signal(barrier, inc=1, device_id=(me, z + 1), device_id_type=MESH)

    def other(o):
        return lax.rem(my + o[0], GY) * GX + lax.rem(mx + o[1], GX)

    @pl.when(is_solver)
    def _():
        for o in OFFSETS:
            pl.semaphore_signal(barrier, inc=1, device_id=(other(o), z), device_id_type=MESH)

    def put(part, plane):
        for s in range(SLOTS):
            a_send[s, part] = plane[WIDE * s : WIDE * (s + 1)]

    zero = jnp.zeros((ROWS, 128), F32)

    def eliminate(i, state):
        link, mass, mass_p = state
        k_next = 0.5 * k[i]
        gi = reciprocal((k_next + mass) + link)
        left = link * gi
        right = k_next * gi
        fl[i - 1] = left
        fr[i] = right
        g[i - 1] = gi
        return link * right, 1.0 + right * mass, mass_p + left * mass

    loads[0].wait()
    state = (0.5 * k[0], zero + 1.0, zero)
    for i in range(1, STEP):
        state = eliminate(i, state)
    state = planes_loop(STEP, PART, eliminate, state)
    for c in range(1, len(parts)):
        loads[c].wait()
        state = planes_loop(PART * c, PART * (c + 1), eliminate, state)
    link, mass, mass_p = state
    fr[0] = zero
    fl[L - 1] = zero
    g[L - 1] = zero
    put(0, mass_p)
    put(1, mass)
    put(2, link)

    loads[first_y].wait()
    loads[first_y + 1].wait()
    row = lax.broadcasted_iota(jnp.int32, (ROWS, 128), 0)
    lane = lax.broadcasted_iota(jnp.int32, (ROWS, 128), 1)
    kya = jnp.where(row == ROWS - 1, 0.0, pltpu.roll(ky[...], ROWS - 1, 0))
    kza = jnp.where(lane == 127, 0.0, pltpu.roll(kz[...], 127, 1))
    planes[0] = 2.0 - ky[...] - kya - kz[...] - kza
    planes[1] = jnp.where(row == 0, 0.0, ky[...])
    planes[2] = kya
    planes[3] = jnp.where(lane == 0, 0.0, kz[...])
    planes[4] = kza

    row8 = lax.broadcasted_iota(jnp.int32, (8, 128), 0)
    tiles = range(ROWS // 8)

    def source(j, state):
        r, r_p = list(state[: len(tiles)]), list(state[len(tiles) :])
        ids = [STEP * j + i for i in range(STEP)]
        v = [[u[i, pl.ds(8 * t, 8)] for t in tiles] for i in ids]
        from_above_row = [[pltpu.roll(v_t, 7, 0) for v_t in v_i] for v_i in v]
        from_below_row = [[pltpu.roll(v_t, 1, 0) for v_t in v_i] for v_i in v]
        for t in tiles:
            rows = pl.ds(8 * t, 8)
            c = [planes[n, rows] for n in range(5)]
            for n, i in enumerate(ids):
                x = v[n][t]
                below = from_below_row[n]
                above = from_above_row[n]
                below = below[t] if t == 0 else jnp.where(row8 == 0, below[t - 1], below[t])
                above = above[t] if t == tiles[-1] else jnp.where(row8 == 7, above[t + 1], above[t])
                b = c[0] * x + c[1] * below + c[2] * above
                b = b + c[3] * pltpu.roll(x, 1, 1) + c[4] * pltpu.roll(x, 127, 1)
                r[t] = b + fr[i, rows] * r[t]
                rg[i, rows] = r[t] * g[i, rows]
                r_p[t] = r_p[t] + fl[i, rows] * r[t]
        return (*r, *r_p)

    state = (jnp.zeros((8, 128), F32),) * (2 * len(tiles))
    for c in range(len(parts)):
        loads[first_u + c].wait()
        state = lax.fori_loop(c * PART // STEP, (c + 1) * PART // STEP, source, state)
    for t in tiles:
        for h in range(8 // WIDE):
            rows = slice(WIDE * h, WIDE * (h + 1))
            a_send[t * (8 // WIDE) + h, 3] = state[len(tiles) + t][rows]
            a_send[t * (8 // WIDE) + h, 4] = state[t][rows]

    for i in range(L):
        send_up[pl.ds(i, 1), :] = u[i, pl.ds(ROWS - 1, 1), :]
        send_down[pl.ds(i, 1), :] = u[i, pl.ds(0, 1), :]
    send_down[pl.ds(L, 8), :] = jnp.broadcast_to(ky[pl.ds(0, 1), :], (8, 128))
    up = pltpu.make_async_remote_copy(
        src_ref=send_up, dst_ref=from_below, send_sem=halo_send_sem.at[0],
        recv_sem=halo_recv_sem.at[0], device_id=(me, z + 1), device_id_type=MESH,
    )
    down = pltpu.make_async_remote_copy(
        src_ref=send_down, dst_ref=from_above, send_sem=halo_send_sem.at[1],
        recv_sem=halo_recv_sem.at[1], device_id=(me, z - 1), device_id_type=MESH,
    )

    @pl.when(z == 0)
    def _():
        from_below[...] = jnp.zeros((L, 128), F32)

    @pl.when(z == NYZ - 1)
    def _():
        from_above[...] = jnp.zeros((L + 8, 128), F32)

    greeted = jnp.where(z > 0, 1, 0) + jnp.where(z < NYZ - 1, 1, 0)
    greeted = greeted + jnp.where(is_solver, len(SOLVERS) - 1, len(SOLVERS))
    pl.semaphore_wait(barrier, greeted)
    pl.when(z < NYZ - 1)(up.start)
    pl.when(z > 0)(down.start)

    def send_slot(s, low, count):
        part = pl.ds(low, count)

        @pl.when(me != SOLVERS[s])
        def _():
            pltpu.make_async_remote_copy(
                src_ref=a_send.at[s, part], dst_ref=a_recv.at[me, part], send_sem=a_send_sem,
                recv_sem=a_recv_sem, device_id=(SOLVERS[s], z), device_id_type=MESH,
            ).start()

        @pl.when(me == SOLVERS[s])
        def _():
            a_recv[me, part] = a_send[s, part]

    for s in range(SLOTS - 2, 0, -1):
        send_slot(s, 0, 5)
    send_slot(0, 0, 3)
    send_slot(SLOTS - 1, 0, 3)

    @pl.when(z > 0)
    def _():
        up.wait_recv()

    @pl.when(z < NYZ - 1)
    def _():
        down.wait_recv()

    c_first = jnp.where(row8 == 0, jnp.broadcast_to(ky[pl.ds(0, 1), :], (8, 128)), 0.0)
    c_last = jnp.where(row8 == 7, from_above[pl.ds(32, 8), :], 0.0)
    first, last = pl.ds(0, 8), pl.ds(ROWS - 8, 8)

    def edge_source(i, state):
        r0, r7, p0, p7 = state
        b0 = c_first * from_below[pl.ds(i, 1), :]
        b7 = c_last * (from_above[pl.ds(i, 1), :] - u[i, last])
        r0 = b0 + fr[i, first] * r0
        r7 = b7 + fr[i, last] * r7
        rg[i, first] += r0 * g[i, first]
        rg[i, last] += r7 * g[i, last]
        return r0, r7, p0 + fl[i, first] * r0, p7 + fl[i, last] * r7

    zero8 = jnp.zeros((8, 128), F32)
    r0, r7, p0, p7 = planes_loop(0, L, edge_source, (zero8,) * 4)
    a_send[0, 3] += p0[:WIDE]
    a_send[0, 4] += r0[:WIDE]
    a_send[SLOTS - 1, 3] += p7[8 - WIDE :]
    a_send[SLOTS - 1, 4] += r7[8 - WIDE :]
    send_slot(0, 3, 2)
    send_slot(SLOTS - 1, 3, 2)

    @pl.when(is_solver)
    def _():
        landed = a_recv.at[pl.ds(0, NG - 1)]
        pltpu.make_async_copy(landed, landed, a_recv_sem).wait()
        masses = [a_recv[d, 1] + (a_recv[d + 1, 0] if d < NG - 1 else 0.0) for d in range(NG)]
        sources = [a_recv[d, 4] + (a_recv[d + 1, 3] if d < NG - 1 else 0.0) for d in range(NG)]
        links = [a_recv[d, 2] for d in range(NG)]
        ids = list(range(NG))
        levels = []
        while len(ids) > 1:
            gone = []
            new_links = []
            for j in range(0, len(ids), 2):
                gi = reciprocal((links[j] + links[j + 1]) + masses[j])
                left, right = links[j] * gi, links[j + 1] * gi
                gone.append((ids[j], left, right, sources[j] * gi))
                if j > 0:
                    masses[j - 1] = masses[j - 1] + left * masses[j]
                    sources[j - 1] = sources[j - 1] + left * sources[j]
                masses[j + 1] = masses[j + 1] + right * masses[j]
                sources[j + 1] = sources[j + 1] + right * sources[j]
                new_links.append(links[j] * right)
            levels.append((gone, ids[1::2]))
            ids, masses, sources, links = ids[1::2], masses[1::2], sources[1::2], new_links
        w = {-1: jnp.zeros((WIDE, 128), F32), ids[0]: sources[0] * reciprocal(masses[0] + links[0])}
        for gone, kept in reversed(levels):
            for j, (d, left, right, part) in enumerate(gone):
                below = kept[j - 1] if j > 0 else -1
                w[d] = left * w[below] + right * w[kept[j]] + part
        for d in range(-1, NG):
            w_send[d + 1] = w[d]
        for i in range(NG):
            d = NG // 2 * (i // (NG // 2)) + lax.rem(i + slot, NG // 2)

            @pl.when(d != me)
            def _():
                pltpu.make_async_remote_copy(
                    src_ref=w_send.at[pl.ds(d, 2)], dst_ref=w_recv.at[slot],
                    send_sem=w_send_sem, recv_sem=w_recv_sem, device_id=(d, z), device_id_type=MESH,
                ).start()

        w_recv[slot] = w_send[pl.ds(me, 2)]
        landed = w_recv.at[pl.ds(0, SLOTS - 1)]
        pltpu.make_async_copy(landed, landed, w_recv_sem).wait()

    @pl.when(jnp.logical_not(is_solver))
    def _():
        pltpu.make_async_copy(w_recv, w_recv, w_recv_sem).wait()

    for s in range(SLOTS):
        planes[0, pl.ds(WIDE * s, WIDE)] = w_recv[s, 0]
        planes[1, pl.ds(WIDE * s, WIDE)] = w_recv[s, 1]
    w_p = planes[0]
    w_last = planes[1]
    def back(j, w):
        i = L - 1 - j
        w = (fl[i] * w_p + rg[i]) + fr[i + 1] * w
        out[i] = w - u[i]
        return w

    out[L - 1] = w_last - u[L - 1]
    w = w_last
    for j in range(1, STEP):
        w = back(j, w)
    planes_loop(STEP, L, back, w)

    @pl.when(z < NYZ - 1)
    def _():
        up.wait_send()

    @pl.when(z > 0)
    def _():
        down.wait_send()

    @pl.when(is_solver)
    def _():
        sent = a_send.at[pl.ds(0, SLOTS - 1)]
        pltpu.make_async_copy(sent, sent, a_send_sem).wait()
        sent = a_recv.at[pl.ds(0, NG - 1), pl.ds(0, 2)]
        pltpu.make_async_copy(sent, sent, w_send_sem).wait()

    @pl.when(jnp.logical_not(is_solver))
    def _():
        pltpu.make_async_copy(a_send, a_send, a_send_sem).wait()


def shards(u, kx, ky, kz):
    field = pltpu.VMEM((L, ROWS, 128), F32)
    any_space = pl.BlockSpec(memory_space=pl.ANY)
    return pl.pallas_call(
        sweep_kernel,
        out_shape=pltpu.VMEM((L, ROWS, 128), F32),
        in_specs=[any_space] * 4,
        out_specs=pl.BlockSpec(memory_space=pltpu.VMEM),
        scratch_shapes=[
            field, field, pltpu.VMEM((ROWS, 128), F32), pltpu.VMEM((ROWS, 128), F32),
            field, field, field, field,
            pltpu.VMEM((5, ROWS, 128), F32),
            pltpu.VMEM((L, 128), F32), pltpu.VMEM((L + 8, 128), F32),
            pltpu.VMEM((L, 128), F32), pltpu.VMEM((L + 8, 128), F32),
            pltpu.VMEM((SLOTS, 5, WIDE, 128), F32), pltpu.VMEM((NG, 5, WIDE, 128), F32),
            pltpu.VMEM((NG + 1, WIDE, 128), F32), pltpu.VMEM((SLOTS, 2, WIDE, 128), F32),
            pltpu.SemaphoreType.DMA((2 + 2 * (L // PART),)), pltpu.SemaphoreType.DMA((2,)),
            pltpu.SemaphoreType.DMA((2,)),
            pltpu.SemaphoreType.DMA, pltpu.SemaphoreType.DMA,
            pltpu.SemaphoreType.DMA, pltpu.SemaphoreType.DMA,
        ],
        compiler_params=pltpu.CompilerParams(
            collective_id=0, has_side_effects=True, vmem_limit_bytes=32 * 1024 * 1024
        ),
        name="implicit_sweep",
    )(*(pltpu.with_memory_space_constraint(a, pltpu.HBM) for a in (u, kx, ky, kz)))


def solution(mesh):
    return jax.shard_map(
        shards,
        mesh=mesh,
        in_specs=(P("gx", "yz", None), P("gx", "yz", None), P("yz", None), P("yz", None)),
        out_specs=P("gx", "yz", None),
        check_vma=False,
    )
```

```python
import functools

import jax
import jax.numpy as jnp
from jax import lax
from jax.experimental import pallas as pl
from jax.experimental.pallas import tpu as pltpu
from jax.sharding import PartitionSpec as P

MESH = pl.DeviceIdType.MESH
F32 = jnp.float32

NG = 32
NYZ = 16
GY, GX = 8, 4
L = 32
ROWS = 64
SLOTS = 16
WIDE = ROWS // SLOTS
PART = 8
STEP = 4


def ring_distance(a, n):
    return min(a, n - a)


SOLVERS = (4, 1, 3, 8, 24, 29, 6, 9, 11, 12, 20, 25, 27, 30, 5, 28)


OFFSETS = sorted(
    [(dy, dx) for dy in range(GY) for dx in range(GX) if (dy, dx) != (0, 0)],
    key=lambda o: -(ring_distance(o[0], GY) + ring_distance(o[1], GX)),
)


def reciprocal(x):
    g = pl.reciprocal(x, approx=True)
    return g * (2.0 - x * g)


def planes_loop(low, high, body, state):
    def step(j, state):
        for i in range(STEP):
            state = body(low + STEP * j + i, state)
        return state

    return lax.fori_loop(0, (high - low) // STEP, step, state)


def sweep_kernel(
    u_hbm, k_hbm, ky_hbm, kz_hbm,
    u, fl, fr, rg, w,
    k, ky, kz, g, planes,
    send_up, send_down, from_below, from_above,
    a_send, a_recv, w_send, w_recv,
    load_sem, halo_send_sem, halo_recv_sem,
    a_send_sem, a_recv_sem, w_send_sem, w_recv_sem,
):
    me = lax.axis_index("gx")
    z = lax.axis_index("yz")
    my, mx = me // GX, me % GX
    is_solver = functools.reduce(jnp.logical_or, [me == s for s in SOLVERS])
    slot = sum(jnp.where(me == d, s, 0) for s, d in enumerate(SOLVERS))
    barrier = pltpu.get_barrier_semaphore()

    parts = [pl.ds(c, PART) for c in range(0, L, PART)]
    pieces = [(k_hbm.at[c], k.at[c]) for c in parts] + [(ky_hbm, ky), (kz_hbm, kz)]
    pieces += [(u_hbm.at[c], u.at[c]) for c in parts]
    loads = [pltpu.make_async_copy(s, d, load_sem.at[i]) for i, (s, d) in enumerate(pieces)]
    for c in loads:
        c.start()
    first_y, first_u = len(parts), len(parts) + 2

    @pl.when(z > 0)
    def _():
        pl.semaphore_signal(barrier, inc=1, device_id=(me, z - 1), device_id_type=MESH)

    @pl.when(z < NYZ - 1)
    def _():
        pl.semaphore_signal(barrier, inc=1, device_id=(me, z + 1), device_id_type=MESH)

    def other(o):
        return lax.rem(my + o[0], GY) * GX + lax.rem(mx + o[1], GX)

    @pl.when(is_solver)
    def _():
        for o in OFFSETS:
            pl.semaphore_signal(barrier, inc=1, device_id=(other(o), z), device_id_type=MESH)

    def put(part, plane):
        for s in range(SLOTS):
            a_send[s, part] = plane[WIDE * s : WIDE * (s + 1)]

    zero = jnp.zeros((ROWS, 128), F32)

    def eliminate(i, state):
        link, mass, mass_p = state
        k_next = 0.5 * k[i]
        gi = reciprocal((k_next + mass) + link)
        left = link * gi
        right = k_next * gi
        fl[i - 1] = left
        fr[i] = right
        g[i - 1] = gi
        return link * right, 1.0 + right * mass, mass_p + left * mass

    loads[0].wait()
    state = (0.5 * k[0], zero + 1.0, zero)
    for i in range(1, STEP):
        state = eliminate(i, state)
    state = planes_loop(STEP, PART, eliminate, state)
    for c in range(1, len(parts)):
        loads[c].wait()
        state = planes_loop(PART * c, PART * (c + 1), eliminate, state)
    link, mass, mass_p = state
    fr[0] = zero
    fl[L - 1] = zero
    g[L - 1] = zero
    put(0, mass_p)
    put(1, mass)
    put(2, link)

    loads[first_y].wait()
    loads[first_y + 1].wait()
    row = lax.broadcasted_iota(jnp.int32, (ROWS, 128), 0)
    lane = lax.broadcasted_iota(jnp.int32, (ROWS, 128), 1)
    kya = jnp.where(row == ROWS - 1, 0.0, pltpu.roll(ky[...], ROWS - 1, 0))
    kza = jnp.where(lane == 127, 0.0, pltpu.roll(kz[...], 127, 1))
    planes[0] = 2.0 - ky[...] - kya - kz[...] - kza
    planes[1] = jnp.where(row == 0, 0.0, ky[...])
    planes[2] = kya
    planes[3] = jnp.where(lane == 0, 0.0, kz[...])
    planes[4] = kza

    row8 = lax.broadcasted_iota(jnp.int32, (8, 128), 0)
    tiles = range(ROWS // 8)

    def source(j, state):
        r, r_p = list(state[: len(tiles)]), list(state[len(tiles) :])
        ids = [STEP * j + i for i in range(STEP)]
        v = [[u[i, pl.ds(8 * t, 8)] for t in tiles] for i in ids]
        from_above_row = [[pltpu.roll(v_t, 7, 0) for v_t in v_i] for v_i in v]
        from_below_row = [[pltpu.roll(v_t, 1, 0) for v_t in v_i] for v_i in v]
        for t in tiles:
            rows = pl.ds(8 * t, 8)
            c = [planes[n, rows] for n in range(5)]
            for n, i in enumerate(ids):
                x = v[n][t]
                below = from_below_row[n]
                above = from_above_row[n]
                below = below[t] if t == 0 else jnp.where(row8 == 0, below[t - 1], below[t])
                above = above[t] if t == tiles[-1] else jnp.where(row8 == 7, above[t + 1], above[t])
                b = c[0] * x + c[1] * below + c[2] * above
                b = b + c[3] * pltpu.roll(x, 1, 1) + c[4] * pltpu.roll(x, 127, 1)
                r[t] = b + fr[i, rows] * r[t]
                rg[i, rows] = r[t] * g[i, rows]
                r_p[t] = r_p[t] + fl[i, rows] * r[t]
        return (*r, *r_p)

    state = (jnp.zeros((8, 128), F32),) * (2 * len(tiles))
    for c in range(len(parts)):
        loads[first_u + c].wait()
        state = lax.fori_loop(c * PART // STEP, (c + 1) * PART // STEP, source, state)
    for t in tiles:
        for h in range(8 // WIDE):
            rows = slice(WIDE * h, WIDE * (h + 1))
            a_send[t * (8 // WIDE) + h, 3] = state[len(tiles) + t][rows]
            a_send[t * (8 // WIDE) + h, 4] = state[t][rows]

    for i in range(L):
        send_up[pl.ds(i, 1), :] = u[i, pl.ds(ROWS - 1, 1), :]
        send_down[pl.ds(i, 1), :] = u[i, pl.ds(0, 1), :]
    send_down[pl.ds(L, 8), :] = jnp.broadcast_to(ky[pl.ds(0, 1), :], (8, 128))
    up = pltpu.make_async_remote_copy(
        src_ref=send_up, dst_ref=from_below, send_sem=halo_send_sem.at[0],
        recv_sem=halo_recv_sem.at[0], device_id=(me, z + 1), device_id_type=MESH,
    )
    down = pltpu.make_async_remote_copy(
        src_ref=send_down, dst_ref=from_above, send_sem=halo_send_sem.at[1],
        recv_sem=halo_recv_sem.at[1], device_id=(me, z - 1), device_id_type=MESH,
    )

    @pl.when(z == 0)
    def _():
        from_below[...] = jnp.zeros((L, 128), F32)

    @pl.when(z == NYZ - 1)
    def _():
        from_above[...] = jnp.zeros((L + 8, 128), F32)

    greeted = jnp.where(z > 0, 1, 0) + jnp.where(z < NYZ - 1, 1, 0)
    greeted = greeted + jnp.where(is_solver, len(SOLVERS) - 1, len(SOLVERS))
    pl.semaphore_wait(barrier, greeted)
    pl.when(z < NYZ - 1)(up.start)
    pl.when(z > 0)(down.start)

    def send_slot(s, low, count):
        part = pl.ds(low, count)

        @pl.when(me != SOLVERS[s])
        def _():
            pltpu.make_async_remote_copy(
                src_ref=a_send.at[s, part], dst_ref=a_recv.at[me, part], send_sem=a_send_sem,
                recv_sem=a_recv_sem, device_id=(SOLVERS[s], z), device_id_type=MESH,
            ).start()

        @pl.when(me == SOLVERS[s])
        def _():
            a_recv[me, part] = a_send[s, part]

    for s in range(SLOTS - 2, 0, -1):
        send_slot(s, 0, 5)
    send_slot(0, 0, 3)
    send_slot(SLOTS - 1, 0, 3)

    @pl.when(z > 0)
    def _():
        up.wait_recv()

    @pl.when(z < NYZ - 1)
    def _():
        down.wait_recv()

    c_first = jnp.where(row8 == 0, jnp.broadcast_to(ky[pl.ds(0, 1), :], (8, 128)), 0.0)
    c_last = jnp.where(row8 == 7, from_above[pl.ds(32, 8), :], 0.0)
    first, last = pl.ds(0, 8), pl.ds(ROWS - 8, 8)

    def edge_source(i, state):
        r0, r7, p0, p7 = state
        b0 = c_first * from_below[pl.ds(i, 1), :]
        b7 = c_last * (from_above[pl.ds(i, 1), :] - u[i, last])
        r0 = b0 + fr[i, first] * r0
        r7 = b7 + fr[i, last] * r7
        rg[i, first] += r0 * g[i, first]
        rg[i, last] += r7 * g[i, last]
        return r0, r7, p0 + fl[i, first] * r0, p7 + fl[i, last] * r7

    zero8 = jnp.zeros((8, 128), F32)
    r0, r7, p0, p7 = planes_loop(0, L, edge_source, (zero8,) * 4)
    a_send[0, 3] += p0[:WIDE]
    a_send[0, 4] += r0[:WIDE]
    a_send[SLOTS - 1, 3] += p7[8 - WIDE :]
    a_send[SLOTS - 1, 4] += r7[8 - WIDE :]
    send_slot(0, 3, 2)
    send_slot(SLOTS - 1, 3, 2)

    @pl.when(is_solver)
    def _():
        landed = a_recv.at[pl.ds(0, NG - 1)]
        pltpu.make_async_copy(landed, landed, a_recv_sem).wait()
        masses = [a_recv[d, 1] + (a_recv[d + 1, 0] if d < NG - 1 else 0.0) for d in range(NG)]
        sources = [a_recv[d, 4] + (a_recv[d + 1, 3] if d < NG - 1 else 0.0) for d in range(NG)]
        links = [a_recv[d, 2] for d in range(NG)]
        ids = list(range(NG))
        levels = []
        while len(ids) > 1:
            gone = []
            new_links = []
            for j in range(0, len(ids), 2):
                gi = reciprocal((links[j] + links[j + 1]) + masses[j])
                left, right = links[j] * gi, links[j + 1] * gi
                gone.append((ids[j], left, right, sources[j] * gi))
                if j > 0:
                    masses[j - 1] = masses[j - 1] + left * masses[j]
                    sources[j - 1] = sources[j - 1] + left * sources[j]
                masses[j + 1] = masses[j + 1] + right * masses[j]
                sources[j + 1] = sources[j + 1] + right * sources[j]
                new_links.append(links[j] * right)
            levels.append((gone, ids[1::2]))
            ids, masses, sources, links = ids[1::2], masses[1::2], sources[1::2], new_links
        value = {-1: jnp.zeros((WIDE, 128), F32), ids[0]: sources[0] * reciprocal(masses[0] + links[0])}
        for gone, kept in reversed(levels):
            for j, (d, left, right, part) in enumerate(gone):
                below = kept[j - 1] if j > 0 else -1
                value[d] = left * value[below] + right * value[kept[j]] + part
        for d in range(-1, NG):
            w_send[d + 1] = value[d]
        for i in range(NG):
            d = NG // 2 * (i // (NG // 2)) + lax.rem(i + slot, NG // 2)

            @pl.when(d != me)
            def _():
                pltpu.make_async_remote_copy(
                    src_ref=w_send.at[pl.ds(d, 2)], dst_ref=w_recv.at[slot],
                    send_sem=w_send_sem, recv_sem=w_recv_sem, device_id=(d, z), device_id_type=MESH,
                ).start()

        w_recv[slot] = w_send[pl.ds(me, 2)]
        landed = w_recv.at[pl.ds(0, SLOTS - 1)]
        pltpu.make_async_copy(landed, landed, w_recv_sem).wait()

    @pl.when(jnp.logical_not(is_solver))
    def _():
        pltpu.make_async_copy(w_recv, w_recv, w_recv_sem).wait()

    for s in range(SLOTS):
        w[0, pl.ds(WIDE * s, WIDE)] = w_recv[s, 0]
        w[1, pl.ds(WIDE * s, WIDE)] = w_recv[s, 1]

    @pl.when(z < NYZ - 1)
    def _():
        up.wait_send()

    @pl.when(z > 0)
    def _():
        down.wait_send()

    @pl.when(is_solver)
    def _():
        sent = a_send.at[pl.ds(0, SLOTS - 1)]
        pltpu.make_async_copy(sent, sent, a_send_sem).wait()
        sent = a_recv.at[pl.ds(0, NG - 1), pl.ds(0, 2)]
        pltpu.make_async_copy(sent, sent, w_send_sem).wait()

    @pl.when(jnp.logical_not(is_solver))
    def _():
        pltpu.make_async_copy(a_send, a_send, a_send_sem).wait()


def back_kernel(u, fl, fr, rg, w, out_hbm, out, store_sem):
    w_p = w[0]

    def back(i, value):
        value = (fl[i] * w_p + rg[i]) + fr[i + 1] * value
        out[i] = value - u[i]
        return value

    value = w[1]
    out[L - 1] = value - u[L - 1]
    stores = []
    for low in range(L - PART, -1, -PART):
        top = low + PART - 1
        if top == L - 1:
            for i in range(top - 1, top - STEP, -1):
                value = back(i, value)
            top -= STEP

        def step(j, value):
            for i in range(STEP):
                value = back(top - STEP * j - i, value)
            return value

        value = lax.fori_loop(0, (top + 1 - low) // STEP, step, value)
        part = pl.ds(low, PART)
        stores.append(pltpu.make_async_copy(out.at[part], out_hbm.at[part], store_sem.at[low // PART]))
        stores[-1].start()
    for c in stores:
        c.wait()


def shards(u, kx, ky, kz):
    shape = (L, ROWS, 128)
    field = pltpu.VMEM(shape, F32)
    plane = pltpu.VMEM((ROWS, 128), F32)
    any_space = pl.BlockSpec(memory_space=pl.ANY)
    vmem = pl.BlockSpec(memory_space=pltpu.VMEM)
    blocks = pl.pallas_call(
        sweep_kernel,
        out_shape=(field, field, field, field, pltpu.VMEM((2, ROWS, 128), F32)),
        in_specs=[any_space] * 4,
        out_specs=(vmem,) * 5,
        scratch_shapes=[
            field, plane, plane, field, pltpu.VMEM((5, ROWS, 128), F32),
            pltpu.VMEM((L, 128), F32), pltpu.VMEM((L + 8, 128), F32),
            pltpu.VMEM((L, 128), F32), pltpu.VMEM((L + 8, 128), F32),
            pltpu.VMEM((SLOTS, 5, WIDE, 128), F32), pltpu.VMEM((NG, 5, WIDE, 128), F32),
            pltpu.VMEM((NG + 1, WIDE, 128), F32), pltpu.VMEM((SLOTS, 2, WIDE, 128), F32),
            pltpu.SemaphoreType.DMA((2 + 2 * (L // PART),)), pltpu.SemaphoreType.DMA((2,)),
            pltpu.SemaphoreType.DMA((2,)),
            pltpu.SemaphoreType.DMA, pltpu.SemaphoreType.DMA,
            pltpu.SemaphoreType.DMA, pltpu.SemaphoreType.DMA,
        ],
        compiler_params=pltpu.CompilerParams(
            collective_id=0, has_side_effects=True, vmem_limit_bytes=24 * 1024 * 1024
        ),
        name="implicit_sweep",
    )(*(pltpu.with_memory_space_constraint(a, pltpu.HBM) for a in (u, kx, ky, kz)))
    return pl.pallas_call(
        back_kernel,
        out_shape=pltpu.HBM(shape, F32),
        in_specs=[vmem] * 5,
        out_specs=any_space,
        scratch_shapes=[field, pltpu.SemaphoreType.DMA((L // PART,))],
        compiler_params=pltpu.CompilerParams(vmem_limit_bytes=16 * 1024 * 1024),
        name="back_substitution",
    )(*(pltpu.with_memory_space_constraint(a, pltpu.VMEM) for a in blocks))


def solution(mesh):
    return jax.shard_map(
        shards,
        mesh=mesh,
        in_specs=(P("gx", "yz", None), P("gx", "yz", None), P("yz", None), P("yz", None)),
        out_specs=P("gx", "yz", None),
        check_vma=False,
    )
```

```python
import functools

import jax
import jax.numpy as jnp
from jax import lax
from jax.experimental import pallas as pl
from jax.experimental.pallas import tpu as pltpu
from jax.sharding import PartitionSpec as P

MESH = pl.DeviceIdType.MESH
F32 = jnp.float32

NG = 32
NYZ = 16
GY, GX = 8, 4
L = 32
ROWS = 64
SLOTS = 16
WIDE = ROWS // SLOTS
PART = 8
STEP = 4


def ring_distance(a, n):
    return min(a, n - a)


SOLVERS = (1, 4, 28, 2, 24, 29, 6, 9, 11, 12, 20, 25, 16, 15, 13, 3)


OFFSETS = sorted(
    [(dy, dx) for dy in range(GY) for dx in range(GX) if (dy, dx) != (0, 0)],
    key=lambda o: -(ring_distance(o[0], GY) + ring_distance(o[1], GX)),
)


def reciprocal(x):
    g = pl.reciprocal(x, approx=True)
    return g * (2.0 - x * g)


def planes_loop(low, high, body, state):
    def step(j, state):
        for i in range(STEP):
            state = body(low + STEP * j + i, state)
        return state

    return lax.fori_loop(0, (high - low) // STEP, step, state)


def sweep_kernel(
    u_hbm, k_hbm, ky_hbm, kz_hbm,
    u, fl, fr, rg, w,
    k, ky, kz, g, planes,
    send_up, send_down, from_below, from_above,
    a_send, a_recv, w_send, w_recv,
    load_sem, halo_send_sem, halo_recv_sem,
    a_send_sem, a_recv_sem, w_send_sem, w_recv_sem,
):
    me = lax.axis_index("gx")
    z = lax.axis_index("yz")
    my, mx = me // GX, me % GX
    is_solver = functools.reduce(jnp.logical_or, [me == s for s in SOLVERS])
    slot = sum(jnp.where(me == d, s, 0) for s, d in enumerate(SOLVERS))
    barrier = pltpu.get_barrier_semaphore()

    parts = [pl.ds(c, PART) for c in range(0, L, PART)]
    pieces = [(k_hbm.at[c], k.at[c]) for c in parts] + [(ky_hbm, ky), (kz_hbm, kz)]
    pieces += [(u_hbm.at[c], u.at[c]) for c in parts]
    loads = [pltpu.make_async_copy(s, d, load_sem.at[i]) for i, (s, d) in enumerate(pieces)]
    for c in loads:
        c.start()
    first_y, first_u = len(parts), len(parts) + 2

    @pl.when(z > 0)
    def _():
        pl.semaphore_signal(barrier, inc=1, device_id=(me, z - 1), device_id_type=MESH)

    @pl.when(z < NYZ - 1)
    def _():
        pl.semaphore_signal(barrier, inc=1, device_id=(me, z + 1), device_id_type=MESH)

    def other(o):
        return lax.rem(my + o[0], GY) * GX + lax.rem(mx + o[1], GX)

    @pl.when(is_solver)
    def _():
        for o in OFFSETS:
            pl.semaphore_signal(barrier, inc=1, device_id=(other(o), z), device_id_type=MESH)

    def put(part, plane):
        for s in range(SLOTS):
            a_send[s, part] = plane[WIDE * s : WIDE * (s + 1)]

    zero = jnp.zeros((ROWS, 128), F32)

    def eliminate(i, state):
        link, mass, mass_p = state
        k_next = 0.5 * k[i]
        gi = reciprocal((k_next + mass) + link)
        left = link * gi
        right = k_next * gi
        fl[i - 1] = left
        fr[i] = right
        g[i - 1] = gi
        return link * right, 1.0 + right * mass, mass_p + left * mass

    loads[0].wait()
    state = (0.5 * k[0], zero + 1.0, zero)
    for i in range(1, STEP):
        state = eliminate(i, state)
    state = planes_loop(STEP, PART, eliminate, state)
    for c in range(1, len(parts)):
        loads[c].wait()
        state = planes_loop(PART * c, PART * (c + 1), eliminate, state)
    link, mass, mass_p = state
    fr[0] = zero
    fl[L - 1] = zero
    g[L - 1] = zero
    put(0, mass_p)
    put(1, mass)
    put(2, link)

    loads[first_y].wait()
    loads[first_y + 1].wait()
    row = lax.broadcasted_iota(jnp.int32, (ROWS, 128), 0)
    lane = lax.broadcasted_iota(jnp.int32, (ROWS, 128), 1)
    kya = jnp.where(row == ROWS - 1, 0.0, pltpu.roll(ky[...], ROWS - 1, 0))
    kza = jnp.where(lane == 127, 0.0, pltpu.roll(kz[...], 127, 1))
    planes[0] = 2.0 - ky[...] - kya - kz[...] - kza
    planes[1] = jnp.where(row == 0, 0.0, ky[...])
    planes[2] = kya
    planes[3] = jnp.where(lane == 0, 0.0, kz[...])
    planes[4] = kza

    row8 = lax.broadcasted_iota(jnp.int32, (8, 128), 0)
    tiles = range(ROWS // 8)

    def source(j, state):
        r, r_p = list(state[: len(tiles)]), list(state[len(tiles) :])
        ids = [STEP * j + i for i in range(STEP)]
        v = [[u[i, pl.ds(8 * t, 8)] for t in tiles] for i in ids]
        from_above_row = [[pltpu.roll(v_t, 7, 0) for v_t in v_i] for v_i in v]
        from_below_row = [[pltpu.roll(v_t, 1, 0) for v_t in v_i] for v_i in v]
        for t in tiles:
            rows = pl.ds(8 * t, 8)
            c = [planes[n, rows] for n in range(5)]
            for n, i in enumerate(ids):
                x = v[n][t]
                below = from_below_row[n]
                above = from_above_row[n]
                below = below[t] if t == 0 else jnp.where(row8 == 0, below[t - 1], below[t])
                above = above[t] if t == tiles[-1] else jnp.where(row8 == 7, above[t + 1], above[t])
                b = c[0] * x + c[1] * below + c[2] * above
                b = b + c[3] * pltpu.roll(x, 1, 1) + c[4] * pltpu.roll(x, 127, 1)
                r[t] = b + fr[i, rows] * r[t]
                rg[i, rows] = r[t] * g[i, rows]
                r_p[t] = r_p[t] + fl[i, rows] * r[t]
        return (*r, *r_p)

    state = (jnp.zeros((8, 128), F32),) * (2 * len(tiles))
    for c in range(len(parts)):
        loads[first_u + c].wait()
        state = lax.fori_loop(c * PART // STEP, (c + 1) * PART // STEP, source, state)
    for t in tiles:
        for h in range(8 // WIDE):
            rows = slice(WIDE * h, WIDE * (h + 1))
            a_send[t * (8 // WIDE) + h, 3] = state[len(tiles) + t][rows]
            a_send[t * (8 // WIDE) + h, 4] = state[t][rows]

    for i in range(L):
        send_up[pl.ds(i, 1), :] = u[i, pl.ds(ROWS - 1, 1), :]
        send_down[pl.ds(i, 1), :] = u[i, pl.ds(0, 1), :]
    send_down[pl.ds(L, 8), :] = jnp.broadcast_to(ky[pl.ds(0, 1), :], (8, 128))
    up = pltpu.make_async_remote_copy(
        src_ref=send_up, dst_ref=from_below, send_sem=halo_send_sem.at[0],
        recv_sem=halo_recv_sem.at[0], device_id=(me, z + 1), device_id_type=MESH,
    )
    down = pltpu.make_async_remote_copy(
        src_ref=send_down, dst_ref=from_above, send_sem=halo_send_sem.at[1],
        recv_sem=halo_recv_sem.at[1], device_id=(me, z - 1), device_id_type=MESH,
    )

    @pl.when(z == 0)
    def _():
        from_below[...] = jnp.zeros((L, 128), F32)

    @pl.when(z == NYZ - 1)
    def _():
        from_above[...] = jnp.zeros((L + 8, 128), F32)

    greeted = jnp.where(z > 0, 1, 0) + jnp.where(z < NYZ - 1, 1, 0)
    greeted = greeted + jnp.where(is_solver, len(SOLVERS) - 1, len(SOLVERS))
    pl.semaphore_wait(barrier, greeted)
    pl.when(z < NYZ - 1)(up.start)
    pl.when(z > 0)(down.start)

    def send_slot(s, low, count):
        part = pl.ds(low, count)

        @pl.when(me != SOLVERS[s])
        def _():
            pltpu.make_async_remote_copy(
                src_ref=a_send.at[s, part], dst_ref=a_recv.at[me, part], send_sem=a_send_sem,
                recv_sem=a_recv_sem, device_id=(SOLVERS[s], z), device_id_type=MESH,
            ).start()

        @pl.when(me == SOLVERS[s])
        def _():
            a_recv[me, part] = a_send[s, part]

    for s in range(SLOTS - 2, 0, -1):
        send_slot(s, 0, 5)
    send_slot(0, 0, 3)
    send_slot(SLOTS - 1, 0, 3)

    @pl.when(z > 0)
    def _():
        up.wait_recv()

    @pl.when(z < NYZ - 1)
    def _():
        down.wait_recv()

    c_first = jnp.where(row8 == 0, jnp.broadcast_to(ky[pl.ds(0, 1), :], (8, 128)), 0.0)
    c_last = jnp.where(row8 == 7, from_above[pl.ds(32, 8), :], 0.0)
    first, last = pl.ds(0, 8), pl.ds(ROWS - 8, 8)

    def edge_source(i, state):
        r0, r7, p0, p7 = state
        b0 = c_first * from_below[pl.ds(i, 1), :]
        b7 = c_last * (from_above[pl.ds(i, 1), :] - u[i, last])
        r0 = b0 + fr[i, first] * r0
        r7 = b7 + fr[i, last] * r7
        rg[i, first] += r0 * g[i, first]
        rg[i, last] += r7 * g[i, last]
        return r0, r7, p0 + fl[i, first] * r0, p7 + fl[i, last] * r7

    zero8 = jnp.zeros((8, 128), F32)
    r0, r7, p0, p7 = planes_loop(0, L, edge_source, (zero8,) * 4)
    a_send[0, 3] += p0[:WIDE]
    a_send[0, 4] += r0[:WIDE]
    a_send[SLOTS - 1, 3] += p7[8 - WIDE :]
    a_send[SLOTS - 1, 4] += r7[8 - WIDE :]
    send_slot(0, 3, 2)
    send_slot(SLOTS - 1, 3, 2)

    @pl.when(is_solver)
    def _():
        landed = a_recv.at[pl.ds(0, NG - 1)]
        pltpu.make_async_copy(landed, landed, a_recv_sem).wait()
        masses = [a_recv[d, 1] + (a_recv[d + 1, 0] if d < NG - 1 else 0.0) for d in range(NG)]
        sources = [a_recv[d, 4] + (a_recv[d + 1, 3] if d < NG - 1 else 0.0) for d in range(NG)]
        links = [a_recv[d, 2] for d in range(NG)]
        ids = list(range(NG))
        levels = []
        while len(ids) > 1:
            gone = []
            new_links = []
            for j in range(0, len(ids), 2):
                gi = reciprocal((links[j] + links[j + 1]) + masses[j])
                left, right = links[j] * gi, links[j + 1] * gi
                gone.append((ids[j], left, right, sources[j] * gi))
                if j > 0:
                    masses[j - 1] = masses[j - 1] + left * masses[j]
                    sources[j - 1] = sources[j - 1] + left * sources[j]
                masses[j + 1] = masses[j + 1] + right * masses[j]
                sources[j + 1] = sources[j + 1] + right * sources[j]
                new_links.append(links[j] * right)
            levels.append((gone, ids[1::2]))
            ids, masses, sources, links = ids[1::2], masses[1::2], sources[1::2], new_links
        value = {-1: jnp.zeros((WIDE, 128), F32), ids[0]: sources[0] * reciprocal(masses[0] + links[0])}
        for gone, kept in reversed(levels):
            for j, (d, left, right, part) in enumerate(gone):
                below = kept[j - 1] if j > 0 else -1
                value[d] = left * value[below] + right * value[kept[j]] + part
        for d in range(-1, NG):
            w_send[d + 1] = value[d]
        for i in range(NG):
            d = NG // 2 * (i // (NG // 2)) + lax.rem(i + slot, NG // 2)

            @pl.when(d != me)
            def _():
                pltpu.make_async_remote_copy(
                    src_ref=w_send.at[pl.ds(d, 2)], dst_ref=w_recv.at[slot],
                    send_sem=w_send_sem, recv_sem=w_recv_sem, device_id=(d, z), device_id_type=MESH,
                ).start()

        w_recv[slot] = w_send[pl.ds(me, 2)]
        landed = w_recv.at[pl.ds(0, SLOTS - 1)]
        pltpu.make_async_copy(landed, landed, w_recv_sem).wait()

    @pl.when(jnp.logical_not(is_solver))
    def _():
        pltpu.make_async_copy(w_recv, w_recv, w_recv_sem).wait()

    for s in range(SLOTS):
        w[0, pl.ds(WIDE * s, WIDE)] = w_recv[s, 0]
        w[1, pl.ds(WIDE * s, WIDE)] = w_recv[s, 1]

    @pl.when(z < NYZ - 1)
    def _():
        up.wait_send()

    @pl.when(z > 0)
    def _():
        down.wait_send()

    @pl.when(is_solver)
    def _():
        sent = a_send.at[pl.ds(0, SLOTS - 1)]
        pltpu.make_async_copy(sent, sent, a_send_sem).wait()
        sent = a_recv.at[pl.ds(0, NG - 1), pl.ds(0, 2)]
        pltpu.make_async_copy(sent, sent, w_send_sem).wait()

    @pl.when(jnp.logical_not(is_solver))
    def _():
        pltpu.make_async_copy(a_send, a_send, a_send_sem).wait()


def back_kernel(u, fl, fr, rg, w, out_hbm, out, store_sem):
    w_p = w[0]

    def back(i, value):
        value = (fl[i] * w_p + rg[i]) + fr[i + 1] * value
        out[i] = value - u[i]
        return value

    value = w[1]
    out[L - 1] = value - u[L - 1]
    stores = []
    for low in range(L - PART, -1, -PART):
        top = low + PART - 1
        if top == L - 1:
            for i in range(top - 1, top - STEP, -1):
                value = back(i, value)
            top -= STEP

        def step(j, value):
            for i in range(STEP):
                value = back(top - STEP * j - i, value)
            return value

        value = lax.fori_loop(0, (top + 1 - low) // STEP, step, value)
        part = pl.ds(low, PART)
        stores.append(pltpu.make_async_copy(out.at[part], out_hbm.at[part], store_sem.at[low // PART]))
        stores[-1].start()
    for c in stores:
        c.wait()


def shards(u, kx, ky, kz):
    shape = (L, ROWS, 128)
    field = pltpu.VMEM(shape, F32)
    plane = pltpu.VMEM((ROWS, 128), F32)
    any_space = pl.BlockSpec(memory_space=pl.ANY)
    vmem = pl.BlockSpec(memory_space=pltpu.VMEM)
    blocks = pl.pallas_call(
        sweep_kernel,
        out_shape=(field, field, field, field, pltpu.VMEM((2, ROWS, 128), F32)),
        in_specs=[any_space] * 4,
        out_specs=(vmem,) * 5,
        scratch_shapes=[
            field, plane, plane, field, pltpu.VMEM((5, ROWS, 128), F32),
            pltpu.VMEM((L, 128), F32), pltpu.VMEM((L + 8, 128), F32),
            pltpu.VMEM((L, 128), F32), pltpu.VMEM((L + 8, 128), F32),
            pltpu.VMEM((SLOTS, 5, WIDE, 128), F32), pltpu.VMEM((NG, 5, WIDE, 128), F32),
            pltpu.VMEM((NG + 1, WIDE, 128), F32), pltpu.VMEM((SLOTS, 2, WIDE, 128), F32),
            pltpu.SemaphoreType.DMA((2 + 2 * (L // PART),)), pltpu.SemaphoreType.DMA((2,)),
            pltpu.SemaphoreType.DMA((2,)),
            pltpu.SemaphoreType.DMA, pltpu.SemaphoreType.DMA,
            pltpu.SemaphoreType.DMA, pltpu.SemaphoreType.DMA,
        ],
        compiler_params=pltpu.CompilerParams(
            collective_id=0, has_side_effects=True, vmem_limit_bytes=24 * 1024 * 1024
        ),
        name="implicit_sweep",
    )(*(pltpu.with_memory_space_constraint(a, pltpu.HBM) for a in (u, kx, ky, kz)))
    return pl.pallas_call(
        back_kernel,
        out_shape=pltpu.HBM(shape, F32),
        in_specs=[vmem] * 5,
        out_specs=any_space,
        scratch_shapes=[field, pltpu.SemaphoreType.DMA((L // PART,))],
        compiler_params=pltpu.CompilerParams(vmem_limit_bytes=16 * 1024 * 1024),
        name="back_substitution",
    )(*(pltpu.with_memory_space_constraint(a, pltpu.VMEM) for a in blocks))


def solution(mesh):
    return jax.shard_map(
        shards,
        mesh=mesh,
        in_specs=(P("gx", "yz", None), P("gx", "yz", None), P("yz", None), P("yz", None)),
        out_specs=P("gx", "yz", None),
        check_vma=False,
    )
```

```python
import functools

import jax
import jax.numpy as jnp
from jax import lax
from jax.experimental import pallas as pl
from jax.experimental.pallas import tpu as pltpu
from jax.sharding import PartitionSpec as P

MESH = pl.DeviceIdType.MESH
F32 = jnp.float32

NG = 32
NYZ = 16
GY, GX = 8, 4
L = 32
ROWS = 64
SLOTS = 16
WIDE = ROWS // SLOTS
PART = 8
STEP = 4


def ring_distance(a, n):
    return min(a, n - a)


SOLVERS = (1, 4, 28, 2, 24, 29, 6, 9, 11, 12, 20, 25, 16, 10, 13, 3)


OFFSETS = sorted(
    [(dy, dx) for dy in range(GY) for dx in range(GX) if (dy, dx) != (0, 0)],
    key=lambda o: -(ring_distance(o[0], GY) + ring_distance(o[1], GX)),
)


def reciprocal(x):
    g = pl.reciprocal(x, approx=True)
    return g * (2.0 - x * g)


def planes_loop(low, high, body, state):
    def step(j, state):
        for i in range(STEP):
            state = body(low + STEP * j + i, state)
        return state

    return lax.fori_loop(0, (high - low) // STEP, step, state)


def sweep_kernel(
    u_hbm, k_hbm, ky_hbm, kz_hbm,
    u, fl, fr, rg, w,
    k, ky, kz, g, planes,
    send_up, send_down, from_below, from_above,
    a_send, a_recv, w_send, w_recv,
    load_sem, halo_send_sem, halo_recv_sem,
    a_send_sem, a_recv_sem, w_send_sem, w_recv_sem,
):
    me = lax.axis_index("gx")
    z = lax.axis_index("yz")
    my, mx = me // GX, me % GX
    is_solver = functools.reduce(jnp.logical_or, [me == s for s in SOLVERS])
    slot = sum(jnp.where(me == d, s, 0) for s, d in enumerate(SOLVERS))
    barrier = pltpu.get_barrier_semaphore()

    parts = [pl.ds(c, PART) for c in range(0, L, PART)]
    pieces = [(k_hbm.at[c], k.at[c]) for c in parts] + [(ky_hbm, ky), (kz_hbm, kz)]
    pieces += [(u_hbm.at[c], u.at[c]) for c in parts]
    loads = [pltpu.make_async_copy(s, d, load_sem.at[i]) for i, (s, d) in enumerate(pieces)]
    for c in loads:
        c.start()
    first_y, first_u = len(parts), len(parts) + 2

    @pl.when(z > 0)
    def _():
        pl.semaphore_signal(barrier, inc=1, device_id=(me, z - 1), device_id_type=MESH)

    @pl.when(z < NYZ - 1)
    def _():
        pl.semaphore_signal(barrier, inc=1, device_id=(me, z + 1), device_id_type=MESH)

    def other(o):
        return lax.rem(my + o[0], GY) * GX + lax.rem(mx + o[1], GX)

    @pl.when(is_solver)
    def _():
        for o in OFFSETS:
            pl.semaphore_signal(barrier, inc=1, device_id=(other(o), z), device_id_type=MESH)

    def put(part, plane):
        for s in range(SLOTS):
            a_send[s, part] = plane[WIDE * s : WIDE * (s + 1)]

    zero = jnp.zeros((ROWS, 128), F32)

    def eliminate(i, state):
        link, mass, mass_p = state
        k_next = 0.5 * k[i]
        gi = reciprocal((k_next + mass) + link)
        left = link * gi
        right = k_next * gi
        fl[i - 1] = left
        fr[i] = right
        g[i - 1] = gi
        return link * right, 1.0 + right * mass, mass_p + left * mass

    loads[0].wait()
    state = (0.5 * k[0], zero + 1.0, zero)
    for i in range(1, STEP):
        state = eliminate(i, state)
    state = planes_loop(STEP, PART, eliminate, state)
    for c in range(1, len(parts)):
        loads[c].wait()
        state = planes_loop(PART * c, PART * (c + 1), eliminate, state)
    link, mass, mass_p = state
    fr[0] = zero
    fl[L - 1] = zero
    g[L - 1] = zero
    put(0, mass_p)
    put(1, mass)
    put(2, link)

    loads[first_y].wait()
    loads[first_y + 1].wait()
    row = lax.broadcasted_iota(jnp.int32, (ROWS, 128), 0)
    lane = lax.broadcasted_iota(jnp.int32, (ROWS, 128), 1)
    kya = jnp.where(row == ROWS - 1, 0.0, pltpu.roll(ky[...], ROWS - 1, 0))
    kza = jnp.where(lane == 127, 0.0, pltpu.roll(kz[...], 127, 1))
    planes[0] = 2.0 - ky[...] - kya - kz[...] - kza
    planes[1] = jnp.where(row == 0, 0.0, ky[...])
    planes[2] = kya
    planes[3] = jnp.where(lane == 0, 0.0, kz[...])
    planes[4] = kza

    row8 = lax.broadcasted_iota(jnp.int32, (8, 128), 0)
    tiles = range(ROWS // 8)

    def source(j, state):
        r, r_p = list(state[: len(tiles)]), list(state[len(tiles) :])
        ids = [STEP * j + i for i in range(STEP)]
        v = [[u[i, pl.ds(8 * t, 8)] for t in tiles] for i in ids]
        from_above_row = [[pltpu.roll(v_t, 7, 0) for v_t in v_i] for v_i in v]
        from_below_row = [[pltpu.roll(v_t, 1, 0) for v_t in v_i] for v_i in v]
        for t in tiles:
            rows = pl.ds(8 * t, 8)
            c = [planes[n, rows] for n in range(5)]
            for n, i in enumerate(ids):
                x = v[n][t]
                below = from_below_row[n]
                above = from_above_row[n]
                below = below[t] if t == 0 else jnp.where(row8 == 0, below[t - 1], below[t])
                above = above[t] if t == tiles[-1] else jnp.where(row8 == 7, above[t + 1], above[t])
                b = c[0] * x + c[1] * below + c[2] * above
                b = b + c[3] * pltpu.roll(x, 1, 1) + c[4] * pltpu.roll(x, 127, 1)
                r[t] = b + fr[i, rows] * r[t]
                rg[i, rows] = r[t] * g[i, rows]
                r_p[t] = r_p[t] + fl[i, rows] * r[t]
        return (*r, *r_p)

    state = (jnp.zeros((8, 128), F32),) * (2 * len(tiles))
    for c in range(len(parts)):
        loads[first_u + c].wait()
        state = lax.fori_loop(c * PART // STEP, (c + 1) * PART // STEP, source, state)
    for t in tiles:
        for h in range(8 // WIDE):
            rows = slice(WIDE * h, WIDE * (h + 1))
            a_send[t * (8 // WIDE) + h, 3] = state[len(tiles) + t][rows]
            a_send[t * (8 // WIDE) + h, 4] = state[t][rows]

    for i in range(L):
        send_up[pl.ds(i, 1), :] = u[i, pl.ds(ROWS - 1, 1), :]
        send_down[pl.ds(i, 1), :] = u[i, pl.ds(0, 1), :]
    send_down[pl.ds(L, 8), :] = jnp.broadcast_to(ky[pl.ds(0, 1), :], (8, 128))
    up = pltpu.make_async_remote_copy(
        src_ref=send_up, dst_ref=from_below, send_sem=halo_send_sem.at[0],
        recv_sem=halo_recv_sem.at[0], device_id=(me, lax.rem(z + 1, NYZ)), device_id_type=MESH,
    )
    down = pltpu.make_async_remote_copy(
        src_ref=send_down, dst_ref=from_above, send_sem=halo_send_sem.at[1],
        recv_sem=halo_recv_sem.at[1], device_id=(me, lax.rem(z + NYZ - 1, NYZ)), device_id_type=MESH,
    )

    @pl.when(z == 0)
    def _():
        from_below[...] = jnp.zeros((L, 128), F32)

    @pl.when(z == NYZ - 1)
    def _():
        from_above[...] = jnp.zeros((L + 8, 128), F32)

    greeted = jnp.where(z > 0, 1, 0) + jnp.where(z < NYZ - 1, 1, 0)
    greeted = greeted + jnp.where(is_solver, len(SOLVERS) - 1, len(SOLVERS))
    pl.semaphore_wait(barrier, greeted)
    pl.when(z < NYZ - 1)(up.start)
    pl.when(z > 0)(down.start)

    def send_slot(s, low, count):
        part = pl.ds(low, count)

        @pl.when(me != SOLVERS[s])
        def _():
            pltpu.make_async_remote_copy(
                src_ref=a_send.at[s, part], dst_ref=a_recv.at[me, part], send_sem=a_send_sem,
                recv_sem=a_recv_sem, device_id=(SOLVERS[s], z), device_id_type=MESH,
            ).start()

        @pl.when(me == SOLVERS[s])
        def _():
            a_recv[me, part] = a_send[s, part]

    for s in range(SLOTS - 2, 0, -1):
        send_slot(s, 0, 5)
    send_slot(0, 0, 3)
    send_slot(SLOTS - 1, 0, 3)

    @pl.when(z > 0)
    def _():
        up.wait_recv()

    @pl.when(z < NYZ - 1)
    def _():
        down.wait_recv()

    c_first = jnp.where(row8 == 0, jnp.broadcast_to(ky[pl.ds(0, 1), :], (8, 128)), 0.0)
    c_last = jnp.where(row8 == 7, from_above[pl.ds(32, 8), :], 0.0)
    first, last = pl.ds(0, 8), pl.ds(ROWS - 8, 8)

    def edge_source(i, state):
        r0, r7, p0, p7 = state
        b0 = c_first * from_below[pl.ds(i, 1), :]
        b7 = c_last * (from_above[pl.ds(i, 1), :] - u[i, last])
        r0 = b0 + fr[i, first] * r0
        r7 = b7 + fr[i, last] * r7
        rg[i, first] += r0 * g[i, first]
        rg[i, last] += r7 * g[i, last]
        return r0, r7, p0 + fl[i, first] * r0, p7 + fl[i, last] * r7

    zero8 = jnp.zeros((8, 128), F32)
    r0, r7, p0, p7 = planes_loop(0, L, edge_source, (zero8,) * 4)
    a_send[0, 3] += p0[:WIDE]
    a_send[0, 4] += r0[:WIDE]
    a_send[SLOTS - 1, 3] += p7[8 - WIDE :]
    a_send[SLOTS - 1, 4] += r7[8 - WIDE :]
    send_slot(0, 3, 2)
    send_slot(SLOTS - 1, 3, 2)

    @pl.when(is_solver)
    def _():
        landed = a_recv.at[pl.ds(0, NG - 1)]
        pltpu.make_async_copy(landed, landed, a_recv_sem).wait()
        masses = [a_recv[d, 1] + (a_recv[d + 1, 0] if d < NG - 1 else 0.0) for d in range(NG)]
        sources = [a_recv[d, 4] + (a_recv[d + 1, 3] if d < NG - 1 else 0.0) for d in range(NG)]
        links = [a_recv[d, 2] for d in range(NG)]
        ids = list(range(NG))
        levels = []
        while len(ids) > 1:
            gone = []
            new_links = []
            for j in range(0, len(ids), 2):
                gi = reciprocal((links[j] + links[j + 1]) + masses[j])
                left, right = links[j] * gi, links[j + 1] * gi
                gone.append((ids[j], left, right, sources[j] * gi))
                if j > 0:
                    masses[j - 1] = masses[j - 1] + left * masses[j]
                    sources[j - 1] = sources[j - 1] + left * sources[j]
                masses[j + 1] = masses[j + 1] + right * masses[j]
                sources[j + 1] = sources[j + 1] + right * sources[j]
                new_links.append(links[j] * right)
            levels.append((gone, ids[1::2]))
            ids, masses, sources, links = ids[1::2], masses[1::2], sources[1::2], new_links
        value = {-1: jnp.zeros((WIDE, 128), F32), ids[0]: sources[0] * reciprocal(masses[0] + links[0])}
        for gone, kept in reversed(levels):
            for j, (d, left, right, part) in enumerate(gone):
                below = kept[j - 1] if j > 0 else -1
                value[d] = left * value[below] + right * value[kept[j]] + part
        for d in range(-1, NG):
            w_send[d + 1] = value[d]
        for i in range(NG):
            d = NG // 2 * (i // (NG // 2)) + lax.rem(i + slot, NG // 2)

            @pl.when(d != me)
            def _():
                pltpu.make_async_remote_copy(
                    src_ref=w_send.at[pl.ds(d, 2)], dst_ref=w_recv.at[slot],
                    send_sem=w_send_sem, recv_sem=w_recv_sem, device_id=(d, z), device_id_type=MESH,
                ).start()

        w_recv[slot] = w_send[pl.ds(me, 2)]
        landed = w_recv.at[pl.ds(0, SLOTS - 1)]
        pltpu.make_async_copy(landed, landed, w_recv_sem).wait()

    @pl.when(jnp.logical_not(is_solver))
    def _():
        pltpu.make_async_copy(w_recv, w_recv, w_recv_sem).wait()

    for s in range(SLOTS):
        w[0, pl.ds(WIDE * s, WIDE)] = w_recv[s, 0]
        w[1, pl.ds(WIDE * s, WIDE)] = w_recv[s, 1]

    @pl.when(z < NYZ - 1)
    def _():
        up.wait_send()

    @pl.when(z > 0)
    def _():
        down.wait_send()

    @pl.when(is_solver)
    def _():
        sent = a_send.at[pl.ds(0, SLOTS - 1)]
        pltpu.make_async_copy(sent, sent, a_send_sem).wait()
        sent = a_recv.at[pl.ds(0, NG - 1), pl.ds(0, 2)]
        pltpu.make_async_copy(sent, sent, w_send_sem).wait()

    @pl.when(jnp.logical_not(is_solver))
    def _():
        pltpu.make_async_copy(a_send, a_send, a_send_sem).wait()


def back_kernel(u, fl, fr, rg, w, out_hbm, out, store_sem):
    w_p = w[0]

    def back(i, value):
        value = (fl[i] * w_p + rg[i]) + fr[i + 1] * value
        out[i] = value - u[i]
        return value

    value = w[1]
    out[L - 1] = value - u[L - 1]
    stores = []
    for low in range(L - PART, -1, -PART):
        top = low + PART - 1
        if top == L - 1:
            for i in range(top - 1, top - STEP, -1):
                value = back(i, value)
            top -= STEP

        def step(j, value):
            for i in range(STEP):
                value = back(top - STEP * j - i, value)
            return value

        value = lax.fori_loop(0, (top + 1 - low) // STEP, step, value)
        part = pl.ds(low, PART)
        stores.append(pltpu.make_async_copy(out.at[part], out_hbm.at[part], store_sem.at[low // PART]))
        stores[-1].start()
    for c in stores:
        c.wait()


def shards(u, kx, ky, kz):
    shape = (L, ROWS, 128)
    field = pltpu.VMEM(shape, F32)
    plane = pltpu.VMEM((ROWS, 128), F32)
    any_space = pl.BlockSpec(memory_space=pl.ANY)
    vmem = pl.BlockSpec(memory_space=pltpu.VMEM)
    blocks = pl.pallas_call(
        sweep_kernel,
        out_shape=(field, field, field, field, pltpu.VMEM((2, ROWS, 128), F32)),
        in_specs=[any_space] * 4,
        out_specs=(vmem,) * 5,
        scratch_shapes=[
            field, plane, plane, field, pltpu.VMEM((5, ROWS, 128), F32),
            pltpu.VMEM((L, 128), F32), pltpu.VMEM((L + 8, 128), F32),
            pltpu.VMEM((L, 128), F32), pltpu.VMEM((L + 8, 128), F32),
            pltpu.VMEM((SLOTS, 5, WIDE, 128), F32), pltpu.VMEM((NG, 5, WIDE, 128), F32),
            pltpu.VMEM((NG + 1, WIDE, 128), F32), pltpu.VMEM((SLOTS, 2, WIDE, 128), F32),
            pltpu.SemaphoreType.DMA((2 + 2 * (L // PART),)), pltpu.SemaphoreType.DMA((2,)),
            pltpu.SemaphoreType.DMA((2,)),
            pltpu.SemaphoreType.DMA, pltpu.SemaphoreType.DMA,
            pltpu.SemaphoreType.DMA, pltpu.SemaphoreType.DMA,
        ],
        compiler_params=pltpu.CompilerParams(
            collective_id=0, has_side_effects=True, vmem_limit_bytes=24 * 1024 * 1024
        ),
        name="implicit_sweep",
    )(*(pltpu.with_memory_space_constraint(a, pltpu.HBM) for a in (u, kx, ky, kz)))
    return pl.pallas_call(
        back_kernel,
        out_shape=pltpu.HBM(shape, F32),
        in_specs=[vmem] * 5,
        out_specs=any_space,
        scratch_shapes=[field, pltpu.SemaphoreType.DMA((L // PART,))],
        compiler_params=pltpu.CompilerParams(vmem_limit_bytes=16 * 1024 * 1024),
        name="back_substitution",
    )(*(pltpu.with_memory_space_constraint(a, pltpu.VMEM) for a in blocks))


def solution(mesh):
    return jax.shard_map(
        shards,
        mesh=mesh,
        in_specs=(P("gx", "yz", None), P("gx", "yz", None), P("yz", None), P("yz", None)),
        out_specs=P("gx", "yz", None),
        check_vma=False,
    )
```

```python
import functools

import jax
import jax.numpy as jnp
from jax import lax
from jax.experimental import pallas as pl
from jax.experimental.pallas import tpu as pltpu
from jax.sharding import PartitionSpec as P

MESH = pl.DeviceIdType.MESH
F32 = jnp.float32

NG = 32
NYZ = 16
GY, GX = 8, 4
L = 32
ROWS = 64
SLOTS = 16
WIDE = ROWS // SLOTS
PART = 8
STEP = 4


def ring_distance(a, n):
    return min(a, n - a)


SOLVERS = (1, 4, 28, 2, 24, 29, 6, 9, 11, 12, 20, 25, 16, 10, 13, 3)


OFFSETS = sorted(
    [(dy, dx) for dy in range(GY) for dx in range(GX) if (dy, dx) != (0, 0)],
    key=lambda o: -(ring_distance(o[0], GY) + ring_distance(o[1], GX)),
)


def reciprocal(x):
    g = pl.reciprocal(x, approx=True)
    return g * (2.0 - x * g)


def planes_loop(low, high, body, state):
    def step(j, state):
        for i in range(STEP):
            state = body(low + STEP * j + i, state)
        return state

    return lax.fori_loop(0, (high - low) // STEP, step, state)


def sweep_kernel(
    u_hbm, k_hbm, ky_hbm, kz_hbm,
    u, fl, fr, rg, w,
    k, ky, kz, g, planes,
    send_up, send_down, from_below, from_above,
    a_send, a_recv, w_send, w_recv,
    load_sem, halo_send_sem, halo_recv_sem,
    a_send_sem, a_recv_sem, w_send_sem, w_recv_sem,
):
    me = lax.axis_index("gx")
    z = lax.axis_index("yz")
    my, mx = me // GX, me % GX
    is_solver = functools.reduce(jnp.logical_or, [me == s for s in SOLVERS])
    slot = sum(jnp.where(me == d, s, 0) for s, d in enumerate(SOLVERS))
    barrier = pltpu.get_barrier_semaphore()

    parts = [pl.ds(c, PART) for c in range(0, L, PART)]
    pieces = [(k_hbm.at[c], k.at[c]) for c in parts] + [(ky_hbm, ky), (kz_hbm, kz)]
    pieces += [(u_hbm.at[c], u.at[c]) for c in parts]
    loads = [pltpu.make_async_copy(s, d, load_sem.at[i]) for i, (s, d) in enumerate(pieces)]
    for c in loads:
        c.start()
    first_y, first_u = len(parts), len(parts) + 2

    @pl.when(z > 0)
    def _():
        pl.semaphore_signal(barrier, inc=1, device_id=(me, z - 1), device_id_type=MESH)

    @pl.when(z < NYZ - 1)
    def _():
        pl.semaphore_signal(barrier, inc=1, device_id=(me, z + 1), device_id_type=MESH)

    def other(o):
        return lax.rem(my + o[0], GY) * GX + lax.rem(mx + o[1], GX)

    @pl.when(is_solver)
    def _():
        for o in OFFSETS:
            pl.semaphore_signal(barrier, inc=1, device_id=(other(o), z), device_id_type=MESH)

    def put(part, plane):
        for s in range(SLOTS):
            a_send[s, part] = plane[WIDE * s : WIDE * (s + 1)]

    zero = jnp.zeros((ROWS, 128), F32)

    def eliminate(i, state):
        link, mass, mass_p = state
        k_next = 0.5 * k[i]
        gi = reciprocal((k_next + mass) + link)
        left = link * gi
        right = k_next * gi
        fl[i - 1] = left
        fr[i] = right
        g[i - 1] = gi
        return link * right, 1.0 + right * mass, mass_p + left * mass

    loads[0].wait()
    state = (0.5 * k[0], zero + 1.0, zero)
    for i in range(1, STEP):
        state = eliminate(i, state)
    state = planes_loop(STEP, PART, eliminate, state)
    for c in range(1, len(parts)):
        loads[c].wait()
        state = planes_loop(PART * c, PART * (c + 1), eliminate, state)
    link, mass, mass_p = state
    fr[0] = zero
    fl[L - 1] = zero
    g[L - 1] = zero
    put(0, mass_p)
    put(1, mass)
    put(2, link)

    loads[first_y].wait()
    loads[first_y + 1].wait()
    row = lax.broadcasted_iota(jnp.int32, (ROWS, 128), 0)
    lane = lax.broadcasted_iota(jnp.int32, (ROWS, 128), 1)
    kya = jnp.where(row == ROWS - 1, 0.0, pltpu.roll(ky[...], ROWS - 1, 0))
    kza = jnp.where(lane == 127, 0.0, pltpu.roll(kz[...], 127, 1))
    planes[0] = 2.0 - ky[...] - kya - kz[...] - kza
    planes[1] = jnp.where(row == 0, 0.0, ky[...])
    planes[2] = kya
    planes[3] = jnp.where(lane == 0, 0.0, kz[...])
    planes[4] = kza

    row8 = lax.broadcasted_iota(jnp.int32, (8, 128), 0)
    tiles = range(ROWS // 8)

    def source(j, state):
        r, r_p = list(state[: len(tiles)]), list(state[len(tiles) :])
        ids = [STEP * j + i for i in range(STEP)]
        v = [[u[i, pl.ds(8 * t, 8)] for t in tiles] for i in ids]
        from_above_row = [[pltpu.roll(v_t, 7, 0) for v_t in v_i] for v_i in v]
        from_below_row = [[pltpu.roll(v_t, 1, 0) for v_t in v_i] for v_i in v]
        for t in tiles:
            rows = pl.ds(8 * t, 8)
            c = [planes[n, rows] for n in range(5)]
            for n, i in enumerate(ids):
                x = v[n][t]
                below = from_below_row[n]
                above = from_above_row[n]
                below = below[t] if t == 0 else jnp.where(row8 == 0, below[t - 1], below[t])
                above = above[t] if t == tiles[-1] else jnp.where(row8 == 7, above[t + 1], above[t])
                b = c[0] * x + c[1] * below + c[2] * above
                b = b + c[3] * pltpu.roll(x, 1, 1) + c[4] * pltpu.roll(x, 127, 1)
                r[t] = b + fr[i, rows] * r[t]
                rg[i, rows] = r[t] * g[i, rows]
                r_p[t] = r_p[t] + fl[i, rows] * r[t]
        return (*r, *r_p)

    state = (jnp.zeros((8, 128), F32),) * (2 * len(tiles))
    for c in range(len(parts)):
        loads[first_u + c].wait()
        state = lax.fori_loop(c * PART // STEP, (c + 1) * PART // STEP, source, state)
    for t in tiles:
        for h in range(8 // WIDE):
            rows = slice(WIDE * h, WIDE * (h + 1))
            a_send[t * (8 // WIDE) + h, 3] = state[len(tiles) + t][rows]
            a_send[t * (8 // WIDE) + h, 4] = state[t][rows]

    for i in range(L):
        send_up[pl.ds(i, 1), :] = u[i, pl.ds(ROWS - 1, 1), :]
        send_down[pl.ds(i, 1), :] = u[i, pl.ds(0, 1), :]
    send_down[pl.ds(L, 8), :] = jnp.broadcast_to(ky[pl.ds(0, 1), :], (8, 128))
    up = pltpu.make_async_remote_copy(
        src_ref=send_up, dst_ref=from_below, send_sem=halo_send_sem.at[0],
        recv_sem=halo_recv_sem.at[0], device_id=(me, lax.rem(z + 1, NYZ)), device_id_type=MESH,
    )
    down = pltpu.make_async_remote_copy(
        src_ref=send_down, dst_ref=from_above, send_sem=halo_send_sem.at[1],
        recv_sem=halo_recv_sem.at[1], device_id=(me, lax.rem(z + NYZ - 1, NYZ)), device_id_type=MESH,
    )

    @pl.when(z == 0)
    def _():
        from_below[...] = jnp.zeros((L, 128), F32)

    @pl.when(z == NYZ - 1)
    def _():
        from_above[...] = jnp.zeros((L + 8, 128), F32)

    greeted = jnp.where(z > 0, 1, 0) + jnp.where(z < NYZ - 1, 1, 0)
    greeted = greeted + jnp.where(is_solver, len(SOLVERS) - 1, len(SOLVERS))
    pl.semaphore_wait(barrier, greeted)
    pl.when(z < NYZ - 1)(up.start)
    pl.when(z > 0)(down.start)

    def send_slot(s, low, count):
        part = pl.ds(low, count)

        @pl.when(me != SOLVERS[s])
        def _():
            pltpu.make_async_remote_copy(
                src_ref=a_send.at[s, part], dst_ref=a_recv.at[me, part], send_sem=a_send_sem,
                recv_sem=a_recv_sem, device_id=(SOLVERS[s], z), device_id_type=MESH,
            ).start()

        @pl.when(me == SOLVERS[s])
        def _():
            a_recv[me, part] = a_send[s, part]

    for s in range(SLOTS - 2, 0, -1):
        send_slot(s, 0, 5)
    send_slot(0, 0, 3)
    send_slot(SLOTS - 1, 0, 3)

    @pl.when(z > 0)
    def _():
        up.wait_recv()

    @pl.when(z < NYZ - 1)
    def _():
        down.wait_recv()

    c_first = jnp.where(row8 == 0, jnp.broadcast_to(ky[pl.ds(0, 1), :], (8, 128)), 0.0)
    c_last = jnp.where(row8 == 7, from_above[pl.ds(32, 8), :], 0.0)
    first, last = pl.ds(0, 8), pl.ds(ROWS - 8, 8)

    def edge_source(i, state):
        r0, r7, p0, p7 = state
        b0 = c_first * from_below[pl.ds(i, 1), :]
        b7 = c_last * (from_above[pl.ds(i, 1), :] - u[i, last])
        r0 = b0 + fr[i, first] * r0
        r7 = b7 + fr[i, last] * r7
        rg[i, first] += r0 * g[i, first]
        rg[i, last] += r7 * g[i, last]
        return r0, r7, p0 + fl[i, first] * r0, p7 + fl[i, last] * r7

    zero8 = jnp.zeros((8, 128), F32)
    r0, r7, p0, p7 = planes_loop(0, L, edge_source, (zero8,) * 4)
    a_send[0, 3] += p0[:WIDE]
    a_send[0, 4] += r0[:WIDE]
    a_send[SLOTS - 1, 3] += p7[8 - WIDE :]
    a_send[SLOTS - 1, 4] += r7[8 - WIDE :]
    send_slot(0, 3, 2)
    send_slot(SLOTS - 1, 3, 2)

    @pl.when(is_solver)
    def _():
        landed = a_recv.at[pl.ds(0, NG - 1)]
        pltpu.make_async_copy(landed, landed, a_recv_sem).wait()
        masses = [a_recv[d, 1] + (a_recv[d + 1, 0] if d < NG - 1 else 0.0) for d in range(NG)]
        sources = [a_recv[d, 4] + (a_recv[d + 1, 3] if d < NG - 1 else 0.0) for d in range(NG)]
        links = [a_recv[d, 2] for d in range(NG)]
        ids = list(range(NG))
        levels = []
        while len(ids) > 1:
            gone = []
            new_links = []
            for j in range(0, len(ids), 2):
                gi = reciprocal((links[j] + links[j + 1]) + masses[j])
                left, right = links[j] * gi, links[j + 1] * gi
                gone.append((ids[j], left, right, sources[j] * gi))
                if j > 0:
                    masses[j - 1] = masses[j - 1] + left * masses[j]
                    sources[j - 1] = sources[j - 1] + left * sources[j]
                masses[j + 1] = masses[j + 1] + right * masses[j]
                sources[j + 1] = sources[j + 1] + right * sources[j]
                new_links.append(links[j] * right)
            levels.append((gone, ids[1::2]))
            ids, masses, sources, links = ids[1::2], masses[1::2], sources[1::2], new_links
        value = {-1: jnp.zeros((WIDE, 128), F32), ids[0]: sources[0] * reciprocal(masses[0] + links[0])}
        for gone, kept in reversed(levels):
            for j, (d, left, right, part) in enumerate(gone):
                below = kept[j - 1] if j > 0 else -1
                value[d] = left * value[below] + right * value[kept[j]] + part
        for d in range(-1, NG):
            w_send[d + 1] = value[d]
        for i in range(NG):
            d = NG // 2 * (i // (NG // 2)) + lax.rem(i + slot, NG // 2)

            @pl.when(d != me)
            def _():
                pltpu.make_async_remote_copy(
                    src_ref=w_send.at[pl.ds(d, 2)], dst_ref=w_recv.at[slot],
                    send_sem=w_send_sem, recv_sem=w_recv_sem, device_id=(d, z), device_id_type=MESH,
                ).start()

        w_recv[slot] = w_send[pl.ds(me, 2)]
        landed = w_recv.at[pl.ds(0, SLOTS - 1)]
        pltpu.make_async_copy(landed, landed, w_recv_sem).wait()

    @pl.when(jnp.logical_not(is_solver))
    def _():
        pltpu.make_async_copy(w_recv, w_recv, w_recv_sem).wait()

    for s in range(SLOTS):
        w[0, pl.ds(WIDE * s, WIDE)] = w_recv[s, 0]
        w[1, pl.ds(WIDE * s, WIDE)] = w_recv[s, 1]

    @pl.when(z < NYZ - 1)
    def _():
        up.wait_send()

    @pl.when(z > 0)
    def _():
        down.wait_send()

    @pl.when(is_solver)
    def _():
        sent = a_send.at[pl.ds(0, SLOTS - 1)]
        pltpu.make_async_copy(sent, sent, a_send_sem).wait()
        sent = a_recv.at[pl.ds(0, NG - 1), pl.ds(0, 2)]
        pltpu.make_async_copy(sent, sent, w_send_sem).wait()

    @pl.when(jnp.logical_not(is_solver))
    def _():
        pltpu.make_async_copy(a_send, a_send, a_send_sem).wait()


def back_kernel(u, fl, fr, rg, w, out_hbm, out, store_sem):
    w_p = w[0]

    def back(i, value):
        value = (fl[i] * w_p + rg[i]) + fr[i + 1] * value
        out[i] = value - u[i]
        return value

    value = w[1]
    out[L - 1] = value - u[L - 1]
    stores = []
    for low in range(L - STEP, -1, -STEP):
        top = low + STEP - 1
        if top == L - 1:
            for i in range(top - 1, top - STEP, -1):
                value = back(i, value)
            top -= STEP

        def step(j, value):
            for i in range(STEP):
                value = back(top - STEP * j - i, value)
            return value

        value = lax.fori_loop(0, (top + 1 - low) // STEP, step, value)
        part = pl.ds(low, STEP)
        stores.append(pltpu.make_async_copy(out.at[part], out_hbm.at[part], store_sem.at[low // STEP]))
        stores[-1].start()
    for c in stores:
        c.wait()


def shards(u, kx, ky, kz):
    shape = (L, ROWS, 128)
    field = pltpu.VMEM(shape, F32)
    plane = pltpu.VMEM((ROWS, 128), F32)
    any_space = pl.BlockSpec(memory_space=pl.ANY)
    vmem = pl.BlockSpec(memory_space=pltpu.VMEM)
    blocks = pl.pallas_call(
        sweep_kernel,
        out_shape=(field, field, field, field, pltpu.VMEM((2, ROWS, 128), F32)),
        in_specs=[any_space] * 4,
        out_specs=(vmem,) * 5,
        scratch_shapes=[
            field, plane, plane, field, pltpu.VMEM((5, ROWS, 128), F32),
            pltpu.VMEM((L, 128), F32), pltpu.VMEM((L + 8, 128), F32),
            pltpu.VMEM((L, 128), F32), pltpu.VMEM((L + 8, 128), F32),
            pltpu.VMEM((SLOTS, 5, WIDE, 128), F32), pltpu.VMEM((NG, 5, WIDE, 128), F32),
            pltpu.VMEM((NG + 1, WIDE, 128), F32), pltpu.VMEM((SLOTS, 2, WIDE, 128), F32),
            pltpu.SemaphoreType.DMA((2 + 2 * (L // PART),)), pltpu.SemaphoreType.DMA((2,)),
            pltpu.SemaphoreType.DMA((2,)),
            pltpu.SemaphoreType.DMA, pltpu.SemaphoreType.DMA,
            pltpu.SemaphoreType.DMA, pltpu.SemaphoreType.DMA,
        ],
        compiler_params=pltpu.CompilerParams(
            collective_id=0, has_side_effects=True, vmem_limit_bytes=24 * 1024 * 1024
        ),
        name="implicit_sweep",
    )(*(pltpu.with_memory_space_constraint(a, pltpu.HBM) for a in (u, kx, ky, kz)))
    return pl.pallas_call(
        back_kernel,
        out_shape=pltpu.HBM(shape, F32),
        in_specs=[vmem] * 5,
        out_specs=any_space,
        scratch_shapes=[field, pltpu.SemaphoreType.DMA((L // STEP,))],
        compiler_params=pltpu.CompilerParams(vmem_limit_bytes=16 * 1024 * 1024),
        name="back_substitution",
    )(*(pltpu.with_memory_space_constraint(a, pltpu.VMEM) for a in blocks))


def solution(mesh):
    return jax.shard_map(
        shards,
        mesh=mesh,
        in_specs=(P("gx", "yz", None), P("gx", "yz", None), P("yz", None), P("yz", None)),
        out_specs=P("gx", "yz", None),
        check_vma=False,
    )
```
